512 devices in a mesh: dp: 16 (over z), expert: 32 (over x, y, core).
Axes of the slice: x: 4, y: 4, z: 16, core: 2. Of those that a mesh axis runs over, the one named last changes fastest.
Arguments:
- tokens: bfloat16 [1792, 4096], P('expert', 'dp'), may hold values from -6 to 6
- route_ids: int32 [1792, 8], P('expert'), may hold values from 0 to 63, as said below
- route_weights: float32 [1792, 8], P('expert'), may hold values from 0.05 to 0.5
- w_gate: bfloat16 [64, 4096, 768], P('expert', 'dp'), may hold values from -0.09375 to 0.09375
- w_up: bfloat16 [64, 4096, 768], P('expert', 'dp'), may hold values from -0.09375 to 0.09375
- w_down: bfloat16 [64, 768, 4096], P('expert', None, 'dp'), may hold values from -0.21875 to 0.21875
Outputs:
- moe_out: bfloat16 [1792, 4096], P('expert', 'dp')
- expert_loads: int32 [64], P('expert')
The draws below stay inside these ranges and needn't reach their ends.
Inputs may be any that keep to these rules, and one draw needn't show every extreme that they name: `route_ids`: A token's 8 experts differ. Among the 56 tokens of one group no expert is chosen by more than 21 of them, and in every group some expert is chosen by exactly 21.
All inputs are finite; a program needn't handle non-finite values.
Results may differ from the reference program's by a relative error of at most 0.035.
Values may be sent and summed in bfloat16 or wider, within the bound.
No kernel may reach another device: no remote copies, remote signals or barrier semaphores. Data moves between devices by JAX's collectives and lax.ppermute only.
A program may use at most 64 MiB of HBM per device.

```python
import math
import jax
import jax.numpy as jnp
from jax import lax

D = 4096
FF = 768
TOPK = 8
TOK_COL = 56
EXPERTS = 64
SLICE = 256
CAP = 21
TOKENS = 1792
N_DP = 16
N_EXPERT = 32


def draw_route_ids(key, part):
    key = jax.random.fold_in(key, 11)

    def one_group(group):
        group_key = jax.random.fold_in(key, group)
        noise = jax.random.randint(jax.random.fold_in(group_key, 1), (TOK_COL, EXPERTS), 0, 1024)
        favored = jax.random.randint(jax.random.fold_in(group_key, 2), (), 0, EXPERTS)
        order = jax.random.permutation(jax.random.fold_in(group_key, 3), EXPERTS).astype(jnp.int32)
        expert_range = jnp.arange(EXPERTS, dtype=jnp.int32)
        shifted = (expert_range - group * (EXPERTS // N_EXPERT)) % EXPERTS
        prefer = jnp.where(shifted < max(EXPERTS // 4, 1), 768, 0)
        lead = jnp.where(expert_range == favored, 1 << 20, 0)
        scores = (noise + prefer[None, :] + lead[None, :]) * EXPERTS + order[None, :]

        def step(counts, row_scores):
            open_scores = jnp.where(counts < CAP, row_scores, -1 - order)
            picked = lax.top_k(open_scores, TOPK)[1].astype(jnp.int32)
            added = jnp.sum((picked[:, None] == expert_range[None, :]).astype(jnp.int32), axis=0)
            return (counts + added, picked)
        counts_start = jnp.zeros((EXPERTS,), jnp.int32)
        return lax.scan(step, counts_start, scores)[1]
    groups = jnp.arange(N_EXPERT, dtype=jnp.int32)
    routes = jax.vmap(one_group)(groups)
    return routes.reshape(TOKENS, TOPK).astype(jnp.int32)


def steps_of(rng, shape, pieces, least, top_value):
    level, own = 1.0, jax.random.fold_in(rng, 6)
    for dim, shards_of in pieces:
        steps = jnp.exp(jax.random.uniform(jax.random.fold_in(own, dim), (shards_of,), jnp.float32, least / len(pieces), top_value / len(pieces)))
        level = level * jnp.repeat(steps, shape[dim] // shards_of).reshape([-1 if axis == dim else 1 for axis in range(len(shape))])
    return level


def centred(key, dims, scale, limit, split=(), held_as=jnp.bfloat16):
    entries = scale * jax.random.normal(key, dims, jnp.float32)
    if split:
        entries = entries * steps_of(key, dims, split, -0.22, 0.18)
    return jnp.clip(entries, -limit, limit).astype(held_as)


def setup_inputs(seed: int = 0) -> dict:
    seeds = jax.random.split(jax.random.key(seed), 7)
    return {
        "tokens": centred(seeds[0], (TOKENS, D), 1.0, 6.0, ((0, 32), (1, 16))),
        "route_ids": draw_route_ids(jax.random.fold_in(seeds[6], 71), 0),
        "route_weights": jnp.clip(jnp.exp(math.log(0.5) - 2.3025851 * jax.random.uniform(seeds[2], (TOKENS, TOPK), jnp.float32) ** steps_of(seeds[2], (TOKENS, TOPK), ((0, 32),), -0.2, 0.2)), 0.05, 0.5),
        "w_gate": centred(seeds[3], (EXPERTS, D, FF), D ** -0.5, 0.09375, ((0, 32), (1, 16))),
        "w_up": centred(seeds[4], (EXPERTS, D, FF), D ** -0.5, 0.09375, ((0, 32), (1, 16))),
        "w_down": centred(seeds[5], (EXPERTS, FF, D), FF ** -0.5, 0.21875, ((0, 32), (2, 16))),
    }


def slot_positions(route_ids):
    grouped = route_ids.reshape(N_EXPERT, TOK_COL * TOPK)
    one_hot = (grouped[:, :, None] == jnp.arange(EXPERTS, dtype=jnp.int32)[None, None, :]).astype(jnp.int32)
    earlier = jnp.cumsum(one_hot, axis=1) - one_hot
    return jnp.sum(earlier * one_hot, axis=2).reshape(N_EXPERT, TOK_COL, TOPK)


def sliced_sum(buffer, weight):
    parts = jnp.einsum('rkd,kdf->rkf', buffer.astype(jnp.float32), weight.reshape(N_DP, SLICE, FF).astype(jnp.float32))
    rounded = lax.optimization_barrier(parts.astype(jnp.bfloat16))
    return jnp.sum(rounded.astype(jnp.float32), axis=1)


def reference(tokens, route_ids, route_weights, w_gate, w_up, w_down):
    position = slot_positions(route_ids)
    grouped_ids = route_ids.reshape(N_EXPERT, TOK_COL, TOPK)
    grouped_tok = tokens.reshape(N_EXPERT, TOK_COL, D).astype(jnp.float32)
    slot_range = jnp.arange(CAP, dtype=jnp.int32)

    def one_expert(expert_id):
        chosen = (grouped_ids == expert_id)[:, :, :, None] & (position[:, :, :, None] == slot_range[None, None, None, :])
        select = jnp.sum(chosen.astype(jnp.float32), axis=2)
        buffer = jnp.einsum('gtc,gtd->gcd', select, grouped_tok).astype(jnp.bfloat16)
        buffer = buffer.reshape(N_EXPERT * CAP, N_DP, SLICE)
        gate = sliced_sum(buffer, w_gate[expert_id])
        upper = sliced_sum(buffer, w_up[expert_id])
        hidden = (jax.nn.silu(gate) * upper).astype(jnp.bfloat16)
        result = jnp.dot(hidden, w_down[expert_id], preferred_element_type=jnp.float32).astype(jnp.bfloat16)
        return result.reshape(N_EXPERT, CAP, D)

    expert_out = lax.map(one_expert, jnp.arange(EXPERTS, dtype=jnp.int32))
    group_index = jnp.broadcast_to(jnp.arange(N_EXPERT, dtype=jnp.int32)[:, None, None], grouped_ids.shape)
    picked = expert_out[grouped_ids, group_index, position]
    mix_weights = lax.optimization_barrier(route_weights.astype(jnp.bfloat16)).astype(jnp.float32)
    mix_weights = mix_weights.reshape(N_EXPERT, TOK_COL, TOPK)
    combined = jnp.einsum('gts,gtsd->gtd', mix_weights, picked.astype(jnp.float32))
    moe_out = combined.astype(jnp.bfloat16).reshape(TOKENS, D)
    flat_ids = route_ids.reshape(-1)
    expert_loads = jnp.sum((flat_ids[:, None] == jnp.arange(EXPERTS, dtype=jnp.int32)[None, :]).astype(jnp.int32), axis=0)
    return moe_out, expert_loads
```

```python
import functools

import jax
import jax.numpy as jnp
from jax import lax
from jax.experimental import pallas as pl
from jax.experimental.pallas import tpu as pltpu
from jax.sharding import PartitionSpec as P

BF = jnp.bfloat16
F32 = jnp.float32
PIECE = 16
NT = (((1,), (1,)), ((), ()))
PARAMS = pltpu.CompilerParams(vmem_limit_bytes=48 * 1024 * 1024)


def dot(a, b):
    return jnp.dot(a, b, preferred_element_type=F32)


def dot_nt(a, b):
    return lax.dot_general(a, b, NT, preferred_element_type=F32)


def iota(shape, dim):
    return lax.broadcasted_iota(jnp.int32, shape, dim)


def floor_div(value, by, limit):
    shift = 1
    while (1 << shift) < limit * by:
        shift += 1
    return (value * (-(-(1 << shift) // by))) >> shift


class Layout:
    def __init__(self, columns, capacity, exp_dev):
        self.columns, self.capacity, self.exp_dev = columns, capacity, exp_dev
        self.slots = capacity * exp_dev
        self.rows = -(-(self.slots + 1) // 16) * 16
        self.total = columns * self.rows
        self.experts = columns * exp_dev

    def split(self, row):
        block = floor_div(row, self.rows, self.total)
        place = row - block * self.rows
        within = jnp.zeros_like(place)
        for other in range(1, self.exp_dev):
            within = within + (place >= other * self.capacity).astype(jnp.int32)
        return block, place, within, place - within * self.capacity


def positions(ids_ref, lay):
    tokens, top_k = ids_ref.shape
    ids = ids_ref[...]
    lanes = iota((tokens, lay.experts), 1)
    chose = jnp.zeros((tokens, lay.experts), F32)
    for s in range(top_k):
        chose = chose + (ids[:, s : s + 1] == lanes).astype(F32)
    before = (iota((tokens, tokens), 0) > iota((tokens, tokens), 1)).astype(F32).astype(BF)
    rank = dot(before, chose.astype(BF))
    return chose, jnp.where(chose > 0, rank, -1.0)


def dispatch_kernel(lay, ids_ref, tokens_ref, out_ref):
    tokens, width = tokens_ref.shape
    padded = -(-tokens // 8) * 8 + 8
    chose, slot = positions(ids_ref, lay)
    ones = jnp.ones((8, tokens), BF)
    counts = dot(ones, chose.astype(BF))
    counts = jnp.concatenate([counts, jnp.zeros((8, width - lay.experts), F32)], axis=1)
    extended = [tokens_ref[...].astype(F32), counts]
    if padded - 8 > tokens:
        extended.insert(1, jnp.zeros((padded - 8 - tokens, width), F32))
    extended = jnp.concatenate(extended, axis=0).astype(BF)
    slot = jnp.concatenate([slot, jnp.full((padded - tokens, lay.experts), -1.0, F32)], axis=0)
    block, place, within, at = lay.split(iota((lay.total, lay.experts), 0))
    of_row = (block * lay.exp_dev + within == iota((lay.total, lay.experts), 1)).astype(F32).astype(BF)
    row_slot = dot_nt(of_row, slot.astype(BF))
    _, place, _, at = lay.split(iota((lay.total, padded), 0))
    wanted = jnp.where(place < lay.slots, at, 1000).astype(F32)
    lane = iota((lay.total, padded), 1)
    off = jnp.where(lane < padded - 8, row_slot - wanted, (place - lay.slots).astype(F32))
    off = jnp.where(lane <= padded - 8, off, 1.0)
    pick = off == 0.0
    out_ref[...] = dot(pick.astype(F32).astype(BF), extended).astype(BF)


def combine_kernel(lay, ids_ref, weights_ref, back_ref, out_ref):
    tokens, top_k = ids_ref.shape
    ids = ids_ref[...]
    mix = weights_ref[...].astype(BF).astype(F32)
    _, slot = positions(ids_ref, lay)
    lanes = iota((tokens, lay.experts), 1)
    weight = jnp.zeros((tokens, lay.experts), F32)
    for s in range(top_k):
        weight = weight + jnp.where(ids[:, s : s + 1] == lanes, mix[:, s : s + 1], 0.0)
    block, place, within, at = lay.split(iota((lay.experts, lay.total), 1))
    of_row = (block * lay.exp_dev + within == iota((lay.experts, lay.total), 0)).astype(F32).astype(BF)
    row_slot = dot(slot.astype(BF), of_row)
    row_weight = dot(weight.astype(BF), of_row)
    _, place, _, at = lay.split(iota((tokens, lay.total), 1))
    wanted = jnp.where(place < lay.slots, at, 1000).astype(F32)
    matrix = jnp.where(row_slot == wanted, row_weight, 0.0).astype(BF)
    out_ref[...] = dot(matrix, back_ref[...]).astype(BF)


def starts_of(counts, lay):
    columns = lay.columns
    before = (iota((columns, columns), 0) < iota((columns, columns), 1)).astype(F32).astype(BF)
    starts, totals, base = [], [], jnp.zeros((8, 1), F32)
    for count in counts:
        starts.append(dot(count.astype(BF), before) + base)
        total = jnp.sum(count, axis=1, keepdims=True)
        totals.append(total)
        base = base + total
    return starts, totals


def spread(values, of_group, product):
    high = jnp.floor(values * (1.0 / 64.0))
    low = values - 64.0 * high
    return product(high.astype(BF), of_group) * 64.0 + product(low.astype(BF), of_group)


def up_kernel(lay, rows, chunk, me_ref, x_ref, gate_ref, upper_ref, meta_ref, loads_ref, *out_refs):
    exp_dev, width, hidden = gate_ref.shape
    me = me_ref[0]
    x = x_ref[...]
    block, place, within, at = lay.split(iota((8, lay.total), 1))
    group_block = lay.split(iota((lay.columns, lay.total), 1))[0]
    of_group = (group_block == iota((lay.columns, lay.total), 0)).astype(F32).astype(BF)
    counts = []
    for w in range(exp_dev):
        lane = (iota((8, width), 1) == me * exp_dev + w).astype(F32).astype(BF)
        seen = jnp.where(place == lay.slots, dot_nt(lane, x), 0.0)
        counts.append(dot_nt(seen.astype(BF), of_group))
    starts, totals = starts_of(counts, lay)
    target = jnp.full((8, lay.total), -1.0, F32)
    for w in range(exp_dev):
        first = spread(starts[w], of_group, dot)
        count = dot(counts[w].astype(BF), of_group)
        here = (within == w) & (place < lay.slots) & (at.astype(F32) < count)
        target = jnp.where(here, first + at.astype(F32), target)
        meta_ref[w * 8 : w * 8 + 8, 0 : lay.columns] = counts[w]
        loads_ref[w] = jnp.sum(totals[w][0:1, 0:1]).astype(jnp.int32)
    target = target[0:1, :].astype(jnp.int32)
    per = rows // PIECE
    for first in range(0, rows, chunk):
        size = min(chunk, rows - first)
        pick = (iota((size, lay.total), 0) + first == target).astype(F32).astype(BF)
        picked = dot(pick, x)
        row = (iota((size, width), 0) + first).astype(F32)
        low = jnp.zeros((1, 1), F32)
        parts = []
        for w in range(exp_dev):
            high = low + totals[w][0:1, 0:1]
            parts.append(jnp.where((row >= low) & (row < high), picked, 0.0).astype(BF))
            low = high
        for which, ref in enumerate((gate_ref, upper_ref)):
            total = dot(parts[0], ref[0])
            for w in range(1, exp_dev):
                total = total + dot(parts[w], ref[w])
            total = total.astype(BF)
            for piece in range(size // PIECE):
                out_refs[which * per + first // PIECE + piece][...] = total[
                    piece * PIECE : (piece + 1) * PIECE
                ]


def down_kernel(lay, rows, chunk, meta_ref, down_ref, *refs):
    exp_dev, hidden, width = down_ref.shape
    per = rows // PIECE
    summed, out_ref, held_ref = refs[: 2 * per], refs[2 * per], refs[2 * per + 1]
    counts = [meta_ref[w * 8 : w * 8 + 8, 0 : lay.columns] for w in range(exp_dev)]
    starts, totals = starts_of(counts, lay)
    for first in range(0, rows, chunk):
        size = min(chunk, rows - first)
        pieces = range(first // PIECE, (first + size) // PIECE)
        gate = jnp.concatenate([summed[p][...] for p in pieces], axis=0).astype(F32)
        upper = jnp.concatenate([summed[per + p][...] for p in pieces], axis=0).astype(F32)
        inner = (gate / (1.0 + jnp.exp(-gate)) * upper).astype(BF)
        row = (iota((size, width), 0) + first).astype(F32)
        result = dot(inner, down_ref[0])
        low = totals[0][0:1, 0:1]
        for w in range(1, exp_dev):
            result = jnp.where(row >= low, dot(inner, down_ref[w]), result)
            low = low + totals[w][0:1, 0:1]
        held_ref[first : first + size, :] = result.astype(BF)
    held = held_ref[...]
    step = lay.rows * 4 if lay.columns % 4 == 0 else lay.rows
    for top in range(0, lay.total, step):
        block, place, within, at = lay.split(iota((step, 128), 0) + top)
        group_block = lay.split(iota((step, lay.columns), 0) + top)[0]
        of_group = (group_block == iota((step, lay.columns), 1)).astype(F32).astype(BF)

        def product(values, matrix):
            return dot_nt(matrix, jnp.broadcast_to(values[0:1, :].astype(F32), (128, lay.columns)).astype(BF))

        target = jnp.full((step, 128), -1.0, F32)
        for w in range(exp_dev):
            start = spread(starts[w], of_group, product)
            count = product(counts[w], of_group)
            here = (within == w) & (place < lay.slots) & (at.astype(F32) < count)
            target = jnp.where(here, start + at.astype(F32), target)
        target = target.astype(jnp.int32)
        blocks = []
        for left in range(0, rows, 128):
            wide = min(128, rows - left)
            blocks.append((target[:, :wide] == iota((step, wide), 1) + left).astype(F32).astype(BF))
        pick = jnp.concatenate(blocks, axis=1) if len(blocks) > 1 else blocks[0]
        out_ref[top : top + step, :] = dot(pick, held).astype(BF)


def experts(lay, rows, chunk, me, received, w_gate, w_up, w_down):
    exp_dev, width, hidden = w_gate.shape
    per = rows // PIECE
    vmem = pl.BlockSpec(memory_space=pltpu.VMEM)
    smem = pl.BlockSpec(memory_space=pltpu.SMEM)
    meta, loads, *parts = pl.pallas_call(
        functools.partial(up_kernel, lay, rows, chunk),
        out_shape=[
            jax.ShapeDtypeStruct((8 * exp_dev, 128), F32),
            jax.ShapeDtypeStruct((exp_dev,), jnp.int32),
        ]
        + [jax.ShapeDtypeStruct((PIECE, hidden), BF)] * (2 * per),
        in_specs=[smem, vmem, vmem, vmem],
        out_specs=[vmem, smem] + [vmem] * (2 * per),
        compiler_params=PARAMS,
        name="up",
    )(me, received, w_gate, w_up)
    summed = lax.psum(parts, "dp")
    out = pl.pallas_call(
        functools.partial(down_kernel, lay, rows, chunk),
        out_shape=jax.ShapeDtypeStruct((lay.total, width), BF),
        in_specs=[vmem] * (2 + 2 * per),
        out_specs=vmem,
        scratch_shapes=[pltpu.VMEM((rows, width), BF)],
        compiler_params=PARAMS,
        name="down",
    )(meta, w_down, *summed)
    return out, loads


def body(tokens, route_ids, route_weights, w_gate, w_up, w_down):
    columns = lax.axis_size("expert")
    tok_col, top_k = route_ids.shape
    exp_dev = w_gate.shape[0]
    width = tokens.shape[1]
    capacity = min(tok_col, 3 * tok_col * top_k // (exp_dev * columns))
    lay = Layout(columns, capacity, exp_dev)
    sending = pl.pallas_call(
        functools.partial(dispatch_kernel, lay),
        out_shape=jax.ShapeDtypeStruct((lay.total, width), BF),
        compiler_params=PARAMS,
        name="dispatch",
    )(route_ids, tokens)
    received = lax.all_to_all(
        sending.reshape(columns, lay.rows, width), "expert", split_axis=0, concat_axis=0, tiled=True
    ).reshape(lay.total, width)
    me = lax.axis_index("expert").astype(jnp.int32).reshape(1)
    rows = columns * lay.slots
    expert_out, loads = experts(lay, rows, 192, me, received, w_gate, w_up, w_down)
    returned = lax.all_to_all(
        expert_out.reshape(columns, lay.rows, width), "expert", split_axis=0, concat_axis=0, tiled=True
    ).reshape(lay.total, width)
    combined = pl.pallas_call(
        functools.partial(combine_kernel, lay),
        out_shape=jax.ShapeDtypeStruct((tok_col, width), BF),
        compiler_params=PARAMS,
        name="combine",
    )(route_ids, route_weights, returned)
    return combined, loads


def solution(mesh):
    placed = (
        P("expert", "dp"),
        P("expert", None),
        P("expert", None),
        P("expert", "dp", None),
        P("expert", "dp", None),
        P("expert", None, "dp"),
    )
    return jax.shard_map(
        body,
        mesh=mesh,
        in_specs=placed,
        out_specs=(P("expert", "dp"), P("expert")),
        check_vma=False,
    )
```

```python
import functools

import jax
import jax.numpy as jnp
from jax import lax
from jax.experimental import pallas as pl
from jax.experimental.pallas import tpu as pltpu
from jax.sharding import PartitionSpec as P

BF = jnp.bfloat16
F32 = jnp.float32
PIECE = 16
ROWS = 576
CHUNK = 192
NT = (((1,), (1,)), ((), ()))
PARAMS = pltpu.CompilerParams(vmem_limit_bytes=48 * 1024 * 1024)


def dot(a, b):
    return jnp.dot(a, b, preferred_element_type=F32)


def dot_nt(a, b):
    return lax.dot_general(a, b, NT, preferred_element_type=F32)


def iota(shape, dim):
    return lax.broadcasted_iota(jnp.int32, shape, dim)


def floor_div(value, by, limit):
    shift = 1
    while (1 << shift) < limit * by:
        shift += 1
    return (value * (-(-(1 << shift) // by))) >> shift


class Layout:
    def __init__(self, columns, capacity, exp_dev):
        self.columns, self.capacity, self.exp_dev = columns, capacity, exp_dev
        self.slots = capacity * exp_dev
        self.rows = -(-(self.slots + 1) // 16) * 16
        self.total = columns * self.rows
        self.experts = columns * exp_dev

    def split(self, row):
        block = floor_div(row, self.rows, self.total)
        place = row - block * self.rows
        within = jnp.zeros_like(place)
        for other in range(1, self.exp_dev):
            within = within + (place >= other * self.capacity).astype(jnp.int32)
        return block, place, within, place - within * self.capacity


def positions(ids_ref, lay):
    tokens, top_k = ids_ref.shape
    ids = ids_ref[...]
    lanes = iota((tokens, lay.experts), 1)
    chose = jnp.zeros((tokens, lay.experts), F32)
    for s in range(top_k):
        chose = chose + (ids[:, s : s + 1] == lanes).astype(F32)
    before = (iota((tokens, tokens), 0) > iota((tokens, tokens), 1)).astype(F32).astype(BF)
    rank = dot(before, chose.astype(BF))
    return chose, jnp.where(chose > 0, rank, -1.0)


def dispatch_kernel(lay, ids_ref, tokens_ref, out_ref):
    tokens, width = tokens_ref.shape
    padded = -(-tokens // 8) * 8 + 8
    chose, slot = positions(ids_ref, lay)
    ones = jnp.ones((8, tokens), BF)
    counts = dot(ones, chose.astype(BF))
    counts = jnp.concatenate([counts, jnp.zeros((8, width - lay.experts), F32)], axis=1)
    extended = [tokens_ref[...].astype(F32), counts]
    if padded - 8 > tokens:
        extended.insert(1, jnp.zeros((padded - 8 - tokens, width), F32))
    extended = jnp.concatenate(extended, axis=0).astype(BF)
    slot = jnp.concatenate([slot, jnp.full((padded - tokens, lay.experts), -1.0, F32)], axis=0)
    block, place, within, at = lay.split(iota((lay.total, lay.experts), 0))
    of_row = (block * lay.exp_dev + within == iota((lay.total, lay.experts), 1)).astype(F32).astype(BF)
    row_slot = dot_nt(of_row, slot.astype(BF))
    _, place, _, at = lay.split(iota((lay.total, padded), 0))
    wanted = jnp.where(place < lay.slots, at, 1000).astype(F32)
    lane = iota((lay.total, padded), 1)
    off = jnp.where(lane < padded - 8, row_slot - wanted, (place - lay.slots).astype(F32))
    off = jnp.where(lane <= padded - 8, off, 1.0)
    pick = off == 0.0
    out_ref[...] = dot(pick.astype(F32).astype(BF), extended).astype(BF)


def combine_kernel(lay, ids_ref, weights_ref, back_ref, out_ref):
    tokens, top_k = ids_ref.shape
    ids = ids_ref[...]
    mix = weights_ref[...].astype(BF).astype(F32)
    _, slot = positions(ids_ref, lay)
    lanes = iota((tokens, lay.experts), 1)
    weight = jnp.zeros((tokens, lay.experts), F32)
    for s in range(top_k):
        weight = weight + jnp.where(ids[:, s : s + 1] == lanes, mix[:, s : s + 1], 0.0)
    block, place, within, at = lay.split(iota((lay.experts, lay.total), 1))
    of_row = (block * lay.exp_dev + within == iota((lay.experts, lay.total), 0)).astype(F32).astype(BF)
    row_slot = dot(slot.astype(BF), of_row)
    row_weight = dot(weight.astype(BF), of_row)
    _, place, _, at = lay.split(iota((tokens, lay.total), 1))
    wanted = jnp.where(place < lay.slots, at, 1000).astype(F32)
    matrix = jnp.where(row_slot == wanted, row_weight, 0.0).astype(BF)
    out_ref[...] = dot(matrix, back_ref[...]).astype(BF)


def starts_of(counts, lay):
    columns = lay.columns
    before = (iota((columns, columns), 0) < iota((columns, columns), 1)).astype(F32).astype(BF)
    starts, totals, base = [], [], jnp.zeros((8, 1), F32)
    for count in counts:
        starts.append(dot(count.astype(BF), before) + base)
        total = jnp.sum(count, axis=1, keepdims=True)
        totals.append(total)
        base = base + total
    return starts, totals


def spread(values, of_group, product):
    high = jnp.floor(values * (1.0 / 64.0))
    low = values - 64.0 * high
    return product(high.astype(BF), of_group) * 64.0 + product(low.astype(BF), of_group)


def up_kernel(lay, rows, chunk, step_ref, x_ref, gate_ref, upper_ref, meta_ref, loads_ref, *refs):
    exp_dev, width, hidden = gate_ref.shape
    per = rows // PIECE
    out_refs, stage_ref, sems = refs[: 2 * per], refs[2 * per], refs[2 * per + 1]
    me, base = step_ref[0], step_ref[1]
    x = x_ref[...]
    block, place, within, at = lay.split(iota((8, lay.total), 1))
    group_block = lay.split(iota((lay.columns, lay.total), 1))[0]
    of_group = (group_block == iota((lay.columns, lay.total), 0)).astype(F32).astype(BF)
    counts = []
    for w in range(exp_dev):
        lane = (iota((8, width), 1) == me * exp_dev + w).astype(F32).astype(BF)
        seen = jnp.where(place == lay.slots, dot_nt(lane, x), 0.0)
        counts.append(dot_nt(seen.astype(BF), of_group))
    starts, totals = starts_of(counts, lay)
    target = jnp.full((8, lay.total), -1.0, F32)
    for w in range(exp_dev):
        first = spread(starts[w], of_group, dot)
        count = dot(counts[w].astype(BF), of_group)
        here = (within == w) & (place < lay.slots) & (at.astype(F32) < count)
        target = jnp.where(here, first + at.astype(F32), target)
        meta_ref[w * 8 : w * 8 + 8, 0 : lay.columns] = counts[w]
        loads_ref[w] = jnp.sum(totals[w][0:1, 0:1]).astype(jnp.int32)
    every = dot((place == lay.slots).astype(F32).astype(BF), x)
    pair = floor_div(iota((width, 128), 0), exp_dev, width)
    pair = (pair == iota((width, 128), 1)).astype(F32)
    pair = jnp.where(iota((width, 128), 0) < lay.experts, pair, 0.0).astype(BF)
    loads_ref[exp_dev] = jnp.max(spread(every, pair, dot)[0:1, :]).astype(jnp.int32)
    target = target[0:1, :].astype(jnp.int32) - base
    shift = base.astype(F32)
    copies = []
    for first in range(0, rows, chunk):
        size = min(chunk, rows - first)
        pick = (iota((size, lay.total), 0) + first == target).astype(F32).astype(BF)
        picked = dot(pick, x)
        row = (iota((size, width), 0) + first).astype(F32) + shift
        low = jnp.zeros((1, 1), F32)
        parts = []
        for w in range(exp_dev):
            high = low + totals[w][0:1, 0:1]
            parts.append(jnp.where((row >= low) & (row < high), picked, 0.0).astype(BF))
            low = high
        for which, ref in enumerate((gate_ref, upper_ref)):
            total = dot(parts[0], ref[0])
            for w in range(1, exp_dev):
                total = total + dot(parts[w], ref[w])
            stage_ref[which, first : first + size, :] = total.astype(BF)
            for piece in range(first // PIECE, (first + size) // PIECE):
                index = which * per + piece
                copies.append(
                    pltpu.make_async_copy(
                        stage_ref.at[which, pl.ds(piece * PIECE, PIECE)], out_refs[index], sems.at[index]
                    )
                )
                copies[-1].start()
    for copy in copies:
        copy.wait()


def down_kernel(lay, rows, chunk, adds, step_ref, meta_ref, down_ref, *refs):
    exp_dev, hidden, width = down_ref.shape
    per = rows // PIECE
    refs = list(refs)
    before_ref = refs.pop(0) if adds else None
    summed, (out_ref, stage_ref, held_ref, sems) = refs[: 2 * per], refs[2 * per :]
    base = step_ref[1]
    copies = []
    for piece in range(per):
        for which in range(2):
            index = which * per + piece
            copies.append(
                pltpu.make_async_copy(
                    summed[index], stage_ref.at[which, pl.ds(piece * PIECE, PIECE)], sems.at[index]
                )
            )
            copies[-1].start()
    counts = [meta_ref[w * 8 : w * 8 + 8, 0 : lay.columns] for w in range(exp_dev)]
    starts, totals = starts_of(counts, lay)
    shift = base.astype(F32)
    for first in range(0, rows, chunk):
        size = min(chunk, rows - first)
        for copy in copies[2 * (first // PIECE) : 2 * ((first + size) // PIECE)]:
            copy.wait()
        gate = stage_ref[0, first : first + size, :].astype(F32)
        upper = stage_ref[1, first : first + size, :].astype(F32)
        inner = (gate / (1.0 + jnp.exp(-gate)) * upper).astype(BF)
        row = (iota((size, width), 0) + first).astype(F32) + shift
        result = dot(inner, down_ref[0])
        low = totals[0][0:1, 0:1]
        for w in range(1, exp_dev):
            result = jnp.where(row >= low, dot(inner, down_ref[w]), result)
            low = low + totals[w][0:1, 0:1]
        held_ref[first : first + size, :] = result.astype(BF)
    held = held_ref[...]
    step = lay.rows * 4 if lay.columns % 4 == 0 else lay.rows
    for top in range(0, lay.total, step):
        block, place, within, at = lay.split(iota((step, 128), 0) + top)
        group_block = lay.split(iota((step, lay.columns), 0) + top)[0]
        of_group = (group_block == iota((step, lay.columns), 1)).astype(F32).astype(BF)

        def product(values, matrix):
            wide = jnp.broadcast_to(values[0:1, :].astype(F32), (128, lay.columns))
            return dot_nt(matrix, wide.astype(BF))

        target = jnp.full((step, 128), -1.0, F32)
        for w in range(exp_dev):
            start = spread(starts[w], of_group, product)
            count = product(counts[w], of_group)
            here = (within == w) & (place < lay.slots) & (at.astype(F32) < count)
            target = jnp.where(here, start + at.astype(F32), target)
        target = target.astype(jnp.int32) - base
        blocks = []
        for left in range(0, rows, 128):
            wide = min(128, rows - left)
            blocks.append((target[:, :wide] == iota((step, wide), 1) + left).astype(F32).astype(BF))
        pick = jnp.concatenate(blocks, axis=1) if len(blocks) > 1 else blocks[0]
        placed = dot(pick, held)
        if adds:
            placed = placed + before_ref[top : top + step, :].astype(F32)
        out_ref[top : top + step, :] = placed.astype(BF)


def experts(lay, rows, chunk, me, base, before, received, w_gate, w_up, w_down):
    exp_dev, width, hidden = w_gate.shape
    per = rows // PIECE
    vmem = pl.BlockSpec(memory_space=pltpu.VMEM)
    smem = pl.BlockSpec(memory_space=pltpu.SMEM)
    anywhere = pl.BlockSpec(memory_space=pl.ANY)
    step = jnp.stack([me, jnp.asarray(base, jnp.int32)])
    meta, loads, *parts = pl.pallas_call(
        functools.partial(up_kernel, lay, rows, chunk),
        out_shape=[
            jax.ShapeDtypeStruct((8 * exp_dev, 128), F32),
            jax.ShapeDtypeStruct((exp_dev + 1,), jnp.int32),
        ]
        + [jax.ShapeDtypeStruct((PIECE, hidden), BF)] * (2 * per),
        in_specs=[smem, vmem, vmem, vmem],
        out_specs=[vmem, smem] + [anywhere] * (2 * per),
        scratch_shapes=[pltpu.VMEM((2, rows, hidden), BF), pltpu.SemaphoreType.DMA((2 * per,))],
        compiler_params=PARAMS,
        name="up",
    )(step, received, w_gate, w_up)
    summed = lax.psum(parts, "dp")
    adds = before is not None
    out = pl.pallas_call(
        functools.partial(down_kernel, lay, rows, chunk, adds),
        out_shape=jax.ShapeDtypeStruct((lay.total, width), BF),
        in_specs=[smem, vmem, vmem] + [vmem] * adds + [anywhere] * (2 * per),
        out_specs=vmem,
        scratch_shapes=[
            pltpu.VMEM((2, rows, hidden), BF),
            pltpu.VMEM((rows, width), BF),
            pltpu.SemaphoreType.DMA((2 * per,)),
        ],
        compiler_params=PARAMS,
        name="down",
    )(step, meta, w_down, *([before] if adds else []), *summed)
    return out, loads


def body(tokens, route_ids, route_weights, w_gate, w_up, w_down):
    columns = lax.axis_size("expert")
    tok_col, top_k = route_ids.shape
    exp_dev = w_gate.shape[0]
    width = tokens.shape[1]
    capacity = min(tok_col, 3 * tok_col * top_k // (exp_dev * columns))
    lay = Layout(columns, capacity, exp_dev)
    sending = pl.pallas_call(
        functools.partial(dispatch_kernel, lay),
        out_shape=jax.ShapeDtypeStruct((lay.total, width), BF),
        compiler_params=PARAMS,
        name="dispatch",
    )(route_ids, tokens)
    received = lax.all_to_all(
        sending.reshape(columns, lay.rows, width), "expert", split_axis=0, concat_axis=0, tiled=True
    ).reshape(lay.total, width)
    me = lax.axis_index("expert").astype(jnp.int32)
    rows = min(ROWS, columns * lay.slots)
    expert_out, loads = experts(lay, rows, CHUNK, me, 0, None, received, w_gate, w_up, w_down)

    def more(carry):
        return carry[0] < loads[exp_dev]

    def further(carry):
        base, out = carry
        out, _ = experts(lay, rows, CHUNK, me, base, out, received, w_gate, w_up, w_down)
        return base + rows, out

    _, expert_out = lax.while_loop(more, further, (jnp.int32(rows), expert_out))
    returned = lax.all_to_all(
        expert_out.reshape(columns, lay.rows, width), "expert", split_axis=0, concat_axis=0, tiled=True
    ).reshape(lay.total, width)
    combined = pl.pallas_call(
        functools.partial(combine_kernel, lay),
        out_shape=jax.ShapeDtypeStruct((tok_col, width), BF),
        compiler_params=PARAMS,
        name="combine",
    )(route_ids, route_weights, returned)
    return combined, loads[:exp_dev]


def solution(mesh):
    placed = (
        P("expert", "dp"),
        P("expert", None),
        P("expert", None),
        P("expert", "dp", None),
        P("expert", "dp", None),
        P("expert", None, "dp"),
    )
    return jax.shard_map(
        body,
        mesh=mesh,
        in_specs=placed,
        out_specs=(P("expert", "dp"), P("expert")),
        check_vma=False,
    )
```

```python
import functools

import jax
import jax.numpy as jnp
from jax import lax
from jax.experimental import pallas as pl
from jax.experimental.pallas import tpu as pltpu
from jax.sharding import PartitionSpec as P

BF = jnp.bfloat16
F32 = jnp.float32
PIECE = 16
ROWS = 576
CHUNK = 192
NT = (((1,), (1,)), ((), ()))
PARAMS = pltpu.CompilerParams(vmem_limit_bytes=48 * 1024 * 1024)


def dot(a, b):
    return jnp.dot(a, b, preferred_element_type=F32)


def dot_nt(a, b):
    return lax.dot_general(a, b, NT, preferred_element_type=F32)


def iota(shape, dim):
    return lax.broadcasted_iota(jnp.int32, shape, dim)


def floor_div(value, by, limit):
    shift = 1
    while (1 << shift) < limit * by:
        shift += 1
    return (value * (-(-(1 << shift) // by))) >> shift


class Layout:
    def __init__(self, columns, capacity, exp_dev):
        self.columns, self.capacity, self.exp_dev = columns, capacity, exp_dev
        self.slots = capacity * exp_dev
        self.rows = -(-(self.slots + 1) // 16) * 16
        self.total = columns * self.rows
        self.experts = columns * exp_dev

    def split(self, row):
        block = floor_div(row, self.rows, self.total)
        place = row - block * self.rows
        within = jnp.zeros_like(place)
        for other in range(1, self.exp_dev):
            within = within + (place >= other * self.capacity).astype(jnp.int32)
        return block, place, within, place - within * self.capacity


def positions(ids_ref, lay):
    top_k, tokens = ids_ref.shape
    ids = ids_ref[...]
    of = iota((lay.experts, tokens), 0)
    chose = jnp.zeros((lay.experts, tokens), F32)
    for s in range(top_k):
        chose = chose + (ids[s : s + 1, :] == of).astype(F32)
    before = (iota((tokens, tokens), 0) < iota((tokens, tokens), 1)).astype(F32).astype(BF)
    rank = dot(chose.astype(BF), before)
    return chose, jnp.where(chose > 0, rank, -1.0)


def dispatch_kernel(lay, ids_ref, tokens_ref, out_ref):
    tokens, width = tokens_ref.shape
    padded = -(-tokens // 8) * 8 + 8
    chose, slot = positions(ids_ref, lay)
    ones = jnp.ones((8, tokens), BF)
    counts = dot_nt(ones, chose.astype(BF))
    counts = jnp.concatenate([counts, jnp.zeros((8, width - lay.experts), F32)], axis=1)
    extended = [tokens_ref[...].astype(F32), counts]
    if padded - 8 > tokens:
        extended.insert(1, jnp.zeros((padded - 8 - tokens, width), F32))
    extended = jnp.concatenate(extended, axis=0).astype(BF)
    slot = jnp.concatenate([slot, jnp.full((lay.experts, padded - tokens), -1.0, F32)], axis=1)
    block, place, within, at = lay.split(iota((lay.total, lay.experts), 0))
    of_row = (block * lay.exp_dev + within == iota((lay.total, lay.experts), 1)).astype(F32).astype(BF)
    row_slot = dot(of_row, slot.astype(BF))
    _, place, _, at = lay.split(iota((lay.total, padded), 0))
    wanted = jnp.where(place < lay.slots, at, 1000).astype(F32)
    lane = iota((lay.total, padded), 1)
    off = jnp.where(lane < padded - 8, row_slot - wanted, (place - lay.slots).astype(F32))
    off = jnp.where(lane <= padded - 8, off, 1.0)
    pick = off == 0.0
    out_ref[...] = dot(pick.astype(F32).astype(BF), extended).astype(BF)


def combine_kernel(lay, ids_ref, weights_ref, back_ref, out_ref):
    top_k, tokens = ids_ref.shape
    ids = ids_ref[...]
    mix = weights_ref[...].astype(BF).astype(F32)
    _, slot = positions(ids_ref, lay)
    of = iota((lay.experts, tokens), 0)
    weight = jnp.zeros((lay.experts, tokens), F32)
    for s in range(top_k):
        weight = weight + jnp.where(ids[s : s + 1, :] == of, mix[s : s + 1, :], 0.0)
    block, place, within, at = lay.split(iota((lay.experts, lay.total), 1))
    of_row = (block * lay.exp_dev + within == iota((lay.experts, lay.total), 0)).astype(F32).astype(BF)
    row_slot = dot(slot.T.astype(BF), of_row)
    row_weight = dot(weight.T.astype(BF), of_row)
    _, place, _, at = lay.split(iota((tokens, lay.total), 1))
    wanted = jnp.where(place < lay.slots, at, 1000).astype(F32)
    matrix = jnp.where(row_slot == wanted, row_weight, 0.0).astype(BF)
    out_ref[...] = dot(matrix, back_ref[...]).astype(BF)


def starts_of(counts, lay):
    columns = lay.columns
    before = (iota((columns, columns), 0) < iota((columns, columns), 1)).astype(F32).astype(BF)
    starts, totals, base = [], [], jnp.zeros((8, 1), F32)
    for count in counts:
        starts.append(dot(count.astype(BF), before) + base)
        total = jnp.sum(count, axis=1, keepdims=True)
        totals.append(total)
        base = base + total
    return starts, totals


def spread(values, of_group, product):
    high = jnp.floor(values * (1.0 / 64.0))
    low = values - 64.0 * high
    return product(high.astype(BF), of_group) * 64.0 + product(low.astype(BF), of_group)


def up_kernel(lay, rows, chunk, step_ref, x_ref, gate_ref, upper_ref, meta_ref, loads_ref, most_ref, *out_refs):
    exp_dev, width, hidden = gate_ref.shape
    per = rows // PIECE
    me, base = step_ref[0], step_ref[1]
    x = x_ref[...]
    block, place, within, at = lay.split(iota((8, lay.total), 1))
    group_block = lay.split(iota((lay.columns, lay.total), 1))[0]
    of_group = (group_block == iota((lay.columns, lay.total), 0)).astype(F32).astype(BF)
    counts = []
    for w in range(exp_dev):
        lane = (iota((8, width), 1) == me * exp_dev + w).astype(F32).astype(BF)
        seen = jnp.where(place == lay.slots, dot_nt(lane, x), 0.0)
        counts.append(dot_nt(seen.astype(BF), of_group))
    starts, totals = starts_of(counts, lay)
    target = jnp.full((8, lay.total), -1.0, F32)
    for w in range(exp_dev):
        first = spread(starts[w], of_group, dot)
        count = dot(counts[w].astype(BF), of_group)
        here = (within == w) & (place < lay.slots) & (at.astype(F32) < count)
        target = jnp.where(here, first + at.astype(F32), target)
        meta_ref[w * 8 : w * 8 + 8, 0 : lay.columns] = counts[w]
        loads_ref[w] = jnp.sum(totals[w][0:1, 0:1]).astype(jnp.int32)
    every = dot((place == lay.slots).astype(F32).astype(BF), x)
    pair = floor_div(iota((width, 128), 0), exp_dev, width)
    pair = (pair == iota((width, 128), 1)).astype(F32)
    pair = jnp.where(iota((width, 128), 0) < lay.experts, pair, 0.0).astype(BF)
    most_ref[0] = jnp.max(spread(every, pair, dot)[0:1, :]).astype(jnp.int32)
    target = target[0:1, :].astype(jnp.int32) - base
    shift = base.astype(F32)
    for first in range(0, rows, chunk):
        size = min(chunk, rows - first)
        pick = (iota((size, lay.total), 0) + first == target).astype(F32).astype(BF)
        picked = dot(pick, x)
        row = (iota((size, width), 0) + first).astype(F32) + shift
        low = jnp.zeros((1, 1), F32)
        parts = []
        for w in range(exp_dev):
            high = low + totals[w][0:1, 0:1]
            parts.append(jnp.where((row >= low) & (row < high), picked, 0.0).astype(BF))
            low = high
        for which, ref in enumerate((gate_ref, upper_ref)):
            total = dot(parts[0], ref[0])
            for w in range(1, exp_dev):
                total = total + dot(parts[w], ref[w])
            total = total.astype(BF)
            for piece in range(size // PIECE):
                out_refs[which * per + first // PIECE + piece][...] = total[
                    piece * PIECE : (piece + 1) * PIECE
                ]


def down_kernel(lay, rows, chunk, adds, step_ref, meta_ref, down_ref, *refs):
    exp_dev, hidden, width = down_ref.shape
    per = rows // PIECE
    refs = list(refs)
    before_ref = refs.pop(0) if adds else None
    summed, (out_ref, held_ref) = refs[: 2 * per], refs[2 * per :]
    base = step_ref[1]
    counts = [meta_ref[w * 8 : w * 8 + 8, 0 : lay.columns] for w in range(exp_dev)]
    starts, totals = starts_of(counts, lay)
    shift = base.astype(F32)
    for first in range(0, rows, chunk):
        size = min(chunk, rows - first)
        pieces = range(first // PIECE, (first + size) // PIECE)
        gate = jnp.concatenate([summed[p][...] for p in pieces], axis=0).astype(F32)
        upper = jnp.concatenate([summed[per + p][...] for p in pieces], axis=0).astype(F32)
        inner = (gate / (1.0 + jnp.exp(-gate)) * upper).astype(BF)
        row = (iota((size, width), 0) + first).astype(F32) + shift
        result = dot(inner, down_ref[0])
        low = totals[0][0:1, 0:1]
        for w in range(1, exp_dev):
            result = jnp.where(row >= low, dot(inner, down_ref[w]), result)
            low = low + totals[w][0:1, 0:1]
        held_ref[first : first + size, :] = result.astype(BF)
    held = held_ref[...]
    step = lay.rows * 4 if lay.columns % 4 == 0 else lay.rows
    for top in range(0, lay.total, step):
        block, place, within, at = lay.split(iota((step, 128), 0) + top)
        group_block = lay.split(iota((step, lay.columns), 0) + top)[0]
        of_group = (group_block == iota((step, lay.columns), 1)).astype(F32).astype(BF)

        def product(values, matrix):
            wide = jnp.broadcast_to(values[0:1, :].astype(F32), (128, lay.columns))
            return dot_nt(matrix, wide.astype(BF))

        target = jnp.full((step, 128), -1.0, F32)
        for w in range(exp_dev):
            start = spread(starts[w], of_group, product)
            count = product(counts[w], of_group)
            here = (within == w) & (place < lay.slots) & (at.astype(F32) < count)
            target = jnp.where(here, start + at.astype(F32), target)
        target = target.astype(jnp.int32) - base
        blocks = []
        for left in range(0, rows, 128):
            wide = min(128, rows - left)
            blocks.append((target[:, :wide] == iota((step, wide), 1) + left).astype(F32).astype(BF))
        pick = jnp.concatenate(blocks, axis=1) if len(blocks) > 1 else blocks[0]
        placed = dot(pick, held)
        if adds:
            placed = placed + before_ref[top : top + step, :].astype(F32)
        out_ref[top : top + step, :] = placed.astype(BF)


def experts(lay, rows, chunk, me, base, before, received, w_gate, w_up, w_down):
    exp_dev, width, hidden = w_gate.shape
    per = rows // PIECE
    vmem = pl.BlockSpec(memory_space=pltpu.VMEM)
    smem = pl.BlockSpec(memory_space=pltpu.SMEM)
    step = jnp.stack([me, jnp.asarray(base, jnp.int32)])
    meta, loads, most, *parts = pl.pallas_call(
        functools.partial(up_kernel, lay, rows, chunk),
        out_shape=[
            jax.ShapeDtypeStruct((8 * exp_dev, 128), F32),
            jax.ShapeDtypeStruct((exp_dev,), jnp.int32),
            jax.ShapeDtypeStruct((1,), jnp.int32),
        ]
        + [jax.ShapeDtypeStruct((PIECE, hidden), BF)] * (2 * per),
        in_specs=[smem, vmem, vmem, vmem],
        out_specs=[vmem, smem, smem] + [vmem] * (2 * per),
        compiler_params=PARAMS,
        name="up",
    )(step, received, w_gate, w_up)
    summed = lax.psum(parts, "dp")
    adds = before is not None
    out = pl.pallas_call(
        functools.partial(down_kernel, lay, rows, chunk, adds),
        out_shape=jax.ShapeDtypeStruct((lay.total, width), BF),
        in_specs=[smem, vmem, vmem] + [vmem] * adds + [vmem] * (2 * per),
        out_specs=vmem,
        scratch_shapes=[pltpu.VMEM((rows, width), BF)],
        compiler_params=PARAMS,
        name="down",
    )(step, meta, w_down, *([before] if adds else []), *summed)
    return out, loads, most[0]


def body(tokens, route_ids, route_weights, w_gate, w_up, w_down):
    columns = lax.axis_size("expert")
    tok_col, top_k = route_ids.shape
    exp_dev = w_gate.shape[0]
    width = tokens.shape[1]
    capacity = min(tok_col, 3 * tok_col * top_k // (exp_dev * columns))
    lay = Layout(columns, capacity, exp_dev)
    sending = pl.pallas_call(
        functools.partial(dispatch_kernel, lay),
        out_shape=jax.ShapeDtypeStruct((lay.total, width), BF),
        compiler_params=PARAMS,
        name="dispatch",
    )(route_ids.T, tokens)
    received = lax.all_to_all(
        sending.reshape(columns, lay.rows, width), "expert", split_axis=0, concat_axis=0, tiled=True
    ).reshape(lay.total, width)
    me = lax.axis_index("expert").astype(jnp.int32)
    rows = min(ROWS, columns * lay.slots)
    expert_out, loads, most = experts(lay, rows, CHUNK, me, 0, None, received, w_gate, w_up, w_down)

    def more(carry):
        return carry[0] < most

    def further(carry):
        base, out = carry
        out, _, _ = experts(lay, rows, CHUNK, me, base, out, received, w_gate, w_up, w_down)
        return base + rows, out

    _, expert_out = lax.while_loop(more, further, (jnp.int32(rows), expert_out))
    returned = lax.all_to_all(
        expert_out.reshape(columns, lay.rows, width), "expert", split_axis=0, concat_axis=0, tiled=True
    ).reshape(lay.total, width)
    combined = pl.pallas_call(
        functools.partial(combine_kernel, lay),
        out_shape=jax.ShapeDtypeStruct((tok_col, width), BF),
        compiler_params=PARAMS,
        name="combine",
    )(route_ids.T, route_weights.T, returned)
    return combined, loads


def solution(mesh):
    placed = (
        P("expert", "dp"),
        P("expert", None),
        P("expert", None),
        P("expert", "dp", None),
        P("expert", "dp", None),
        P("expert", None, "dp"),
    )
    return jax.shard_map(
        body,
        mesh=mesh,
        in_specs=placed,
        out_specs=(P("expert", "dp"), P("expert")),
        check_vma=False,
    )
```

```python
import functools

import jax
import jax.numpy as jnp
import numpy as np
from jax import lax
from jax.experimental import pallas as pl
from jax.experimental.pallas import tpu as pltpu
from jax.sharding import PartitionSpec as P

BF = jnp.bfloat16
F32 = jnp.float32
PIECE = 16
ROWS = 576
CHUNK = 192
NT = (((1,), (1,)), ((), ()))
PARAMS = pltpu.CompilerParams(vmem_limit_bytes=24 * 1024 * 1024)


def dot(a, b):
    return jnp.dot(a, b, preferred_element_type=F32)


def dot_nt(a, b):
    return lax.dot_general(a, b, NT, preferred_element_type=F32)


def iota(shape, dim):
    return lax.broadcasted_iota(jnp.int32, shape, dim)


FREE, COUNTS = 90, 100


class Layout:
    def __init__(self, columns, capacity, exp_dev):
        self.columns, self.capacity, self.exp_dev = columns, capacity, exp_dev
        self.sub = -(-(capacity + 1) // 8) * 8
        self.rows = -(-(self.sub * exp_dev) // 16) * 16
        self.total = columns * self.rows
        self.experts = columns * exp_dev
        self.wide = -(-(self.experts + 1) // 128) * 128
        row = np.arange(self.total)
        group, place = row // self.rows, row % self.rows
        within = np.minimum(place // self.sub, exp_dev - 1)
        at = place - within * self.sub
        at = np.where(at < capacity, at, np.where((at == capacity) & (within == 0), COUNTS, FREE))
        table = np.zeros((self.total, self.wide), np.float32)
        table[row, within * columns + group] = 1.0
        table[:, self.experts] = -at
        self.table = table

    def expert_ids(self, shape, dim):
        at = iota(shape, dim)
        ids = at * self.exp_dev
        for w in range(1, self.exp_dev):
            ids = ids - jnp.where(at >= w * self.columns, self.experts - 1, 0)
        return ids


def chosen(ids_ref, lay):
    top_k, tokens = ids_ref.shape
    ids = ids_ref[...]
    of = lay.expert_ids((lay.experts, tokens), 0)
    chose = jnp.zeros((lay.experts, tokens), F32)
    for s in range(top_k):
        chose = chose + (ids[s : s + 1, :] == of).astype(F32)
    before = (iota((tokens, tokens), 0) < iota((tokens, tokens), 1)).astype(F32).astype(BF)
    rank = dot(chose.astype(BF), before)
    return chose, jnp.where(chose > 0, rank, -1.0)


def dispatch_kernel(lay, ids_ref, tokens_ref, table_ref, out_ref):
    tokens, width = tokens_ref.shape
    real = -(-tokens // 8) * 8
    chose, slot = chosen(ids_ref, lay)
    counts = dot_nt(jnp.ones((8, tokens), BF), chose.astype(BF))
    counts = jnp.concatenate([counts, jnp.zeros((8, width - lay.experts), F32)], axis=1)
    extended = [tokens_ref[...].astype(F32), counts]
    if real > tokens:
        extended.insert(1, jnp.zeros((real - tokens, width), F32))
    extended = jnp.concatenate(extended, axis=0).astype(BF)
    extra = jnp.where(iota((lay.experts, real + 8 - tokens), 1) == real - tokens, float(COUNTS), -1.0)
    slot = jnp.concatenate([slot, extra], axis=1)
    ones = (iota((lay.wide - lay.experts, real + 8), 0) == 0).astype(F32)
    slot = jnp.concatenate([slot, ones], axis=0).astype(BF)
    pick = (dot(table_ref[...], slot) == 0.0).astype(F32).astype(BF)
    out_ref[...] = dot(pick, extended).astype(BF)


def mix_kernel(lay, ids_ref, weights_ref, across_ref, *refs):
    n = (len(refs) - 2) // 2
    sources, out_ref, held, sems = refs[:n], refs[n], refs[n + 1 : 2 * n + 1], refs[2 * n + 1]
    copies = [pltpu.make_async_copy(a, b, sems.at[i]) for i, (a, b) in enumerate(zip(sources, held))]
    for copy in copies:
        copy.start()
    top_k, tokens = ids_ref.shape
    ids = ids_ref[...]
    mix = weights_ref[...].astype(BF).astype(F32)
    _, slot = chosen(ids_ref, lay)
    of = lay.expert_ids((lay.experts, tokens), 0)
    weight = jnp.zeros((lay.experts, tokens), F32)
    for s in range(top_k):
        weight = weight + jnp.where(ids[s : s + 1, :] == of, mix[s : s + 1, :], 0.0)
    rest = (tokens, lay.wide - lay.experts)
    slot = jnp.concatenate([slot.T, (iota(rest, 1) == 0).astype(F32)], axis=1).astype(BF)
    weight = jnp.concatenate([weight.T, jnp.zeros(rest, F32)], axis=1).astype(BF)
    across = across_ref[...]
    out_ref[...] = jnp.where(dot(slot, across) == 0.0, dot(weight, across), 0.0).astype(BF)
    for copy in copies:
        copy.wait()


def combine_kernel(matrix_ref, back_ref, out_ref):
    out_ref[...] = dot(matrix_ref[...], back_ref[...]).astype(BF)


def starts_of(counts, lay):
    i, k = iota((lay.wide, lay.wide), 0), iota((lay.wide, lay.wide), 1)
    start = dot(counts.astype(BF), (i < k).astype(F32).astype(BF))
    start = jnp.where(iota(start.shape, 1) < lay.experts, start, 0.0)
    high = jnp.floor(start * (1.0 / 64.0))
    return high, start - 64.0 * high


def ends_of(counts, lay):
    lane = iota((1, lay.wide), 1)
    return [
        jnp.sum(jnp.where(lane < (w + 1) * lay.columns, counts[0:1], 0.0), axis=1, keepdims=True)
        for w in range(lay.exp_dev)
    ]


def up_kernel(lay, rows, chunk, step_ref, x_ref, gate_ref, upper_ref, across_ref, meta_ref, loads_ref, most_ref, *out_refs):
    exp_dev, width, hidden = gate_ref.shape
    per = rows // PIECE
    me, base = step_ref[0], step_ref[1]
    x = x_ref[...]
    across = across_ref[...]
    of_group = jnp.where(
        across_ref[lay.experts : lay.experts + 16, :].astype(F32)[0:1, :] == float(-COUNTS),
        across_ref[0 : lay.columns, :].astype(F32),
        0.0,
    ).astype(BF)
    every = dot(of_group, x).astype(BF)
    own = []
    for w in range(exp_dev):
        lane = (iota((8, width), 1) == w * lay.columns + me).astype(F32).astype(BF)
        own.append(dot_nt(lane, every))
    own.append(jnp.zeros((8, lay.wide - lay.experts), F32))
    counts = jnp.concatenate(own, axis=1)
    meta_ref[...] = counts
    high, low = starts_of(counts, lay)
    ends = ends_of(counts, lay)
    lane, row = iota((8, lay.wide), 1), iota((8, lay.wide), 0)
    low = jnp.where(lane == lay.experts, -1.0, low)
    room = jnp.where(lane == lay.experts, 1.0, counts)
    terms = jnp.where(row == 0, high, jnp.where(row == 1, low, room)).astype(BF)
    spread = dot(terms, across)
    target = jnp.where(spread[2:3] > 0.0, 64.0 * spread[0:1] + spread[1:2], -1.0)
    target = target.astype(jnp.int32) - base
    shift = base.astype(F32)
    for first in range(0, rows, chunk):
        size = min(chunk, rows - first)
        pick = (iota((size, lay.total), 0) + first == target).astype(F32).astype(BF)
        picked = dot(pick, x)
        row = (iota((size, width), 0) + first).astype(F32) + shift
        begin = jnp.zeros((1, 1), F32)
        parts = []
        for w in range(exp_dev):
            parts.append(jnp.where((row >= begin) & (row < ends[w]), picked, 0.0).astype(BF))
            begin = ends[w]
        for which, ref in enumerate((gate_ref, upper_ref)):
            total = dot(parts[0], ref[0])
            for w in range(1, exp_dev):
                total = total + dot(parts[w], ref[w])
            total = total.astype(BF)
            for piece in range(size // PIECE):
                out_refs[which * per + first // PIECE + piece][...] = total[
                    piece * PIECE : (piece + 1) * PIECE
                ]
    loads = dot(jnp.ones((8, lay.columns), BF), every)[0:1]
    begin = 0.0
    for w in range(exp_dev):
        loads_ref[w] = (jnp.sum(ends[w]) - begin).astype(jnp.int32)
        begin = jnp.sum(ends[w])
    lane = iota((1, width), 1)
    full = loads
    for w in range(1, exp_dev):
        full = full + pltpu.roll(loads, width - w * lay.columns, axis=1)
    most_ref[0] = jnp.max(jnp.where(lane < lay.columns, full, 0.0)).astype(jnp.int32)


def down_kernel(lay, rows, chunk, adds, step_ref, meta_ref, down_ref, table_ref, *refs):
    exp_dev, hidden, width = down_ref.shape
    per = rows // PIECE
    refs = list(refs)
    before_ref = refs.pop(0) if adds else None
    summed, (out_ref, held_ref) = refs[: 2 * per], refs[2 * per :]
    base = step_ref[1]
    counts = meta_ref[...]
    high, low = starts_of(counts, lay)
    ends = ends_of(counts, lay)
    lane = iota((8, lay.wide), 1)
    low = jnp.where(lane == lay.experts, -1.0, low)
    room = jnp.where(lane == lay.experts, 1.0, counts)
    high, low, room = (jnp.broadcast_to(v[0:1], (128, lay.wide)).astype(BF) for v in (high, low, room))
    shift = base.astype(F32)
    for first in range(0, rows, chunk):
        size = min(chunk, rows - first)
        pieces = range(first // PIECE, (first + size) // PIECE)
        gate = jnp.concatenate([summed[p][...] for p in pieces], axis=0).astype(F32)
        upper = jnp.concatenate([summed[per + p][...] for p in pieces], axis=0).astype(F32)
        inner = (gate / (1.0 + jnp.exp(-gate)) * upper).astype(BF)
        row = (iota((size, width), 0) + first).astype(F32) + shift
        result = dot(inner, down_ref[0])
        for w in range(1, exp_dev):
            result = jnp.where(row >= ends[w - 1], dot(inner, down_ref[w]), result)
        held_ref[first : first + size, :] = result.astype(BF)
    held = held_ref[...]
    step = lay.rows * 4 if lay.columns % 4 == 0 else lay.rows
    for top in range(0, lay.total, step):
        table = table_ref[top : top + step, :]
        target = 64.0 * dot_nt(table, high) + dot_nt(table, low)
        target = jnp.where(dot_nt(table, room) > 0.0, target, -1.0).astype(jnp.int32) - base
        blocks = []
        for left in range(0, rows, 128):
            wide = min(128, rows - left)
            blocks.append((target[:, :wide] == iota((step, wide), 1) + left).astype(F32).astype(BF))
        pick = jnp.concatenate(blocks, axis=1) if len(blocks) > 1 else blocks[0]
        placed = dot(pick, held)
        if adds:
            placed = placed + before_ref[top : top + step, :].astype(F32)
        out_ref[top : top + step, :] = placed.astype(BF)


def experts(lay, rows, chunk, me, base, before, received, w_gate, w_up, w_down):
    exp_dev, width, hidden = w_gate.shape
    per = rows // PIECE
    vmem = pl.BlockSpec(memory_space=pltpu.VMEM)
    smem = pl.BlockSpec(memory_space=pltpu.SMEM)
    step = jnp.stack([me, jnp.asarray(base, jnp.int32)])
    meta, loads, most, *parts = pl.pallas_call(
        functools.partial(up_kernel, lay, rows, chunk),
        out_shape=[
            jax.ShapeDtypeStruct((8, lay.wide), F32),
            jax.ShapeDtypeStruct((exp_dev,), jnp.int32),
            jax.ShapeDtypeStruct((1,), jnp.int32),
        ]
        + [jax.ShapeDtypeStruct((PIECE, hidden), BF)] * (2 * per),
        in_specs=[smem] + [vmem] * 4,
        out_specs=[vmem, smem, smem] + [vmem] * (2 * per),
        compiler_params=PARAMS,
        name="up",
    )(step, received, w_gate, w_up, jnp.asarray(lay.table.T, BF))
    summed = lax.psum(parts, "dp")
    adds = before is not None
    out = pl.pallas_call(
        functools.partial(down_kernel, lay, rows, chunk, adds),
        out_shape=jax.ShapeDtypeStruct((lay.total, width), BF),
        in_specs=[smem] + [vmem] * (3 + adds + 2 * per),
        out_specs=vmem,
        scratch_shapes=[pltpu.VMEM((rows, width), BF)],
        compiler_params=PARAMS,
        name="down",
    )(step, meta, w_down, jnp.asarray(lay.table, BF), *([before] if adds else []), *summed)
    return out, loads, most[0]


def body(tokens, route_ids, route_weights, w_gate, w_up, w_down):
    columns = lax.axis_size("expert")
    tok_col, top_k = route_ids.shape
    exp_dev = w_gate.shape[0]
    width = tokens.shape[1]
    capacity = min(tok_col, 3 * tok_col * top_k // (exp_dev * columns))
    lay = Layout(columns, capacity, exp_dev)
    sending = pl.pallas_call(
        functools.partial(dispatch_kernel, lay),
        out_shape=jax.ShapeDtypeStruct((lay.total, width), BF),
        compiler_params=PARAMS,
        name="dispatch",
    )(route_ids.T, tokens, jnp.asarray(lay.table, BF))
    received = lax.all_to_all(
        sending.reshape(columns, lay.rows, width), "expert", split_axis=0, concat_axis=0, tiled=True
    ).reshape(lay.total, width)
    vmem = pl.BlockSpec(memory_space=pltpu.VMEM)
    weights = (w_gate, w_up)
    matrix, *near = pl.pallas_call(
        functools.partial(mix_kernel, lay),
        out_shape=[jax.ShapeDtypeStruct((tok_col, lay.total), BF)]
        + [jax.ShapeDtypeStruct(w.shape, w.dtype) for w in weights],
        in_specs=[vmem] * 3 + [pl.BlockSpec(memory_space=pl.ANY)] * 2,
        out_specs=[vmem] * 3,
        scratch_shapes=[pltpu.SemaphoreType.DMA((2,))],
        compiler_params=PARAMS,
        name="mix",
    )(route_ids.T, route_weights.T, jnp.asarray(lay.table.T, BF), *weights)
    me = lax.axis_index("expert").astype(jnp.int32)
    rows = min(ROWS, columns * exp_dev * capacity)
    expert_out, loads, most = experts(lay, rows, CHUNK, me, 0, None, received, *near, w_down)

    def more(carry):
        return carry[0] < most

    def further(carry):
        base, out = carry
        out, _, _ = experts(lay, rows, CHUNK, me, base, out, received, w_gate, w_up, w_down)
        return base + rows, out

    _, expert_out = lax.while_loop(more, further, (jnp.int32(rows), expert_out))
    returned = lax.all_to_all(
        expert_out.reshape(columns, lay.rows, width), "expert", split_axis=0, concat_axis=0, tiled=True
    ).reshape(lay.total, width)
    combined = pl.pallas_call(
        combine_kernel,
        out_shape=jax.ShapeDtypeStruct((tok_col, width), BF),
        compiler_params=PARAMS,
        name="combine",
    )(matrix, returned)
    return combined, loads


def solution(mesh):
    placed = (
        P("expert", "dp"),
        P("expert", None),
        P("expert", None),
        P("expert", "dp", None),
        P("expert", "dp", None),
        P("expert", None, "dp"),
    )
    return jax.shard_map(
        body,
        mesh=mesh,
        in_specs=placed,
        out_specs=(P("expert", "dp"), P("expert")),
        check_vma=False,
    )
```

```python
import functools

import jax
import jax.numpy as jnp
import numpy as np
from jax import lax
from jax.experimental import pallas as pl
from jax.experimental.pallas import tpu as pltpu
from jax.sharding import PartitionSpec as P

BF = jnp.bfloat16
F32 = jnp.float32
PIECE = 16
ROWS = 576
CHUNK = 576
NT = (((1,), (1,)), ((), ()))
PARAMS = pltpu.CompilerParams(vmem_limit_bytes=24 * 1024 * 1024)


def dot(a, b):
    return jnp.dot(a, b, preferred_element_type=F32)


def dot_nt(a, b):
    return lax.dot_general(a, b, NT, preferred_element_type=F32)


def iota(shape, dim):
    return lax.broadcasted_iota(jnp.int32, shape, dim)


FREE, COUNTS = 90, 100


class Layout:
    def __init__(self, columns, capacity, exp_dev):
        self.columns, self.capacity, self.exp_dev = columns, capacity, exp_dev
        self.sub = -(-(capacity + 1) // 8) * 8
        self.rows = -(-(self.sub * exp_dev) // 16) * 16
        self.total = columns * self.rows
        self.experts = columns * exp_dev
        self.wide = -(-(self.experts + 1) // 128) * 128
        row = np.arange(self.total)
        group, place = row // self.rows, row % self.rows
        within = np.minimum(place // self.sub, exp_dev - 1)
        at = place - within * self.sub
        at = np.where(at < capacity, at, np.where((at == capacity) & (within == 0), COUNTS, FREE))
        table = np.zeros((self.total, self.wide), np.float32)
        table[row, within * columns + group] = 1.0
        table[:, self.experts] = -at
        self.table = table

    def expert_ids(self, shape, dim):
        at = iota(shape, dim)
        ids = at * self.exp_dev
        for w in range(1, self.exp_dev):
            ids = ids - jnp.where(at >= w * self.columns, self.experts - 1, 0)
        return ids


def chosen(ids_ref, lay):
    top_k, tokens = ids_ref.shape
    ids = ids_ref[...]
    of = lay.expert_ids((lay.experts, tokens), 0)
    chose = jnp.zeros((lay.experts, tokens), F32)
    for s in range(top_k):
        chose = chose + (ids[s : s + 1, :] == of).astype(F32)
    before = (iota((tokens, tokens), 0) < iota((tokens, tokens), 1)).astype(F32).astype(BF)
    rank = dot(chose.astype(BF), before)
    return chose, jnp.where(chose > 0, rank, -1.0)


def dispatch_kernel(lay, ids_from, tokens_from, table_from, out_ref, ids_ref, tokens_ref, table_ref, sems):
    copies = [
        pltpu.make_async_copy(ids_from, ids_ref, sems.at[0]),
        pltpu.make_async_copy(tokens_from, tokens_ref, sems.at[1]),
        pltpu.make_async_copy(table_from, table_ref, sems.at[2]),
    ]
    for copy in copies:
        copy.start()
    copies[0].wait()
    tokens, width = tokens_ref.shape
    real = -(-tokens // 8) * 8
    chose, slot = chosen(ids_ref, lay)
    counts = dot_nt(jnp.ones((8, tokens), BF), chose.astype(BF))
    counts = jnp.concatenate([counts, jnp.zeros((8, width - lay.experts), F32)], axis=1)
    copies[1].wait()
    extended = [tokens_ref[...].astype(F32), counts]
    if real > tokens:
        extended.insert(1, jnp.zeros((real - tokens, width), F32))
    extended = jnp.concatenate(extended, axis=0).astype(BF)
    extra = jnp.where(iota((lay.experts, real + 8 - tokens), 1) == real - tokens, float(COUNTS), -1.0)
    slot = jnp.concatenate([slot, extra], axis=1)
    ones = (iota((lay.wide - lay.experts, real + 8), 0) == 0).astype(F32)
    slot = jnp.concatenate([slot, ones], axis=0).astype(BF)
    copies[2].wait()
    pick = (dot(table_ref[...], slot) == 0.0).astype(F32).astype(BF)
    out_ref[...] = dot(pick, extended).astype(BF)


def mix_kernel(lay, ids_ref, weights_ref, across_ref, out_ref):
    top_k, tokens = ids_ref.shape
    ids = ids_ref[...]
    mix = weights_ref[...].astype(BF).astype(F32)
    _, slot = chosen(ids_ref, lay)
    of = lay.expert_ids((lay.experts, tokens), 0)
    weight = jnp.zeros((lay.experts, tokens), F32)
    for s in range(top_k):
        weight = weight + jnp.where(ids[s : s + 1, :] == of, mix[s : s + 1, :], 0.0)
    rest = (tokens, lay.wide - lay.experts)
    slot = jnp.concatenate([slot.T, (iota(rest, 1) == 0).astype(F32)], axis=1).astype(BF)
    weight = jnp.concatenate([weight.T, jnp.zeros(rest, F32)], axis=1).astype(BF)
    across = across_ref[...]
    out_ref[...] = jnp.where(dot(slot, across) == 0.0, dot(weight, across), 0.0).astype(BF)


def combine_kernel(matrix_ref, back_ref, out_ref):
    out_ref[...] = dot(matrix_ref[...], back_ref[...]).astype(BF)


def starts_of(counts, lay):
    i, k = iota((lay.wide, lay.wide), 0), iota((lay.wide, lay.wide), 1)
    start = dot(counts.astype(BF), (i < k).astype(F32).astype(BF))
    start = jnp.where(iota(start.shape, 1) < lay.experts, start, 0.0)
    high = jnp.floor(start * (1.0 / 64.0))
    return high, start - 64.0 * high


def ends_of(counts, lay):
    lane = iota((1, lay.wide), 1)
    return [
        jnp.sum(jnp.where(lane < (w + 1) * lay.columns, counts[0:1], 0.0), axis=1, keepdims=True)
        for w in range(lay.exp_dev)
    ]


def up_kernel(lay, rows, chunk, step_ref, x_ref, gate_ref, upper_ref, across_ref, meta_ref, loads_ref, most_ref, *out_refs):
    exp_dev, width, hidden = gate_ref.shape
    per = rows // PIECE
    me, base = step_ref[0], step_ref[1]
    x = x_ref[...]
    across = across_ref[...]
    of_group = jnp.where(
        across_ref[lay.experts : lay.experts + 16, :].astype(F32)[0:1, :] == float(-COUNTS),
        across_ref[0 : lay.columns, :].astype(F32),
        0.0,
    ).astype(BF)
    every = dot(of_group, x).astype(BF)
    own = []
    for w in range(exp_dev):
        lane = (iota((8, width), 1) == w * lay.columns + me).astype(F32).astype(BF)
        own.append(dot_nt(lane, every))
    own.append(jnp.zeros((8, lay.wide - lay.experts), F32))
    counts = jnp.concatenate(own, axis=1)
    meta_ref[...] = counts
    high, low = starts_of(counts, lay)
    ends = ends_of(counts, lay)
    lane, row = iota((8, lay.wide), 1), iota((8, lay.wide), 0)
    low = jnp.where(lane == lay.experts, -1.0, low)
    room = jnp.where(lane == lay.experts, 1.0, counts)
    terms = jnp.where(row == 0, high, jnp.where(row == 1, low, room)).astype(BF)
    spread = dot(terms, across)
    target = jnp.where(spread[2:3] > 0.0, 64.0 * spread[0:1] + spread[1:2], -1.0)
    target = target.astype(jnp.int32) - base
    loads = dot(jnp.ones((8, lay.columns), BF), every)[0:1]
    begin = 0.0
    for w in range(exp_dev):
        loads_ref[w] = (jnp.sum(ends[w]) - begin).astype(jnp.int32)
        begin = jnp.sum(ends[w])
    lanes = iota((1, width), 1)
    full = loads
    for w in range(1, exp_dev):
        full = full + pltpu.roll(loads, width - w * lay.columns, axis=1)
    most_ref[0] = jnp.max(jnp.where(lanes < lay.columns, full, 0.0)).astype(jnp.int32)
    shift = base.astype(F32)
    for first in range(0, rows, chunk):
        size = min(chunk, rows - first)
        pick = (iota((size, lay.total), 0) + first == target).astype(F32).astype(BF)
        picked = dot(pick, x)
        row = (iota((size, width), 0) + first).astype(F32) + shift
        begin = jnp.zeros((1, 1), F32)
        parts = []
        for w in range(exp_dev):
            parts.append(jnp.where((row >= begin) & (row < ends[w]), picked, 0.0).astype(BF))
            begin = ends[w]
        parts = jnp.concatenate(parts, axis=1)
        for which, ref in enumerate((gate_ref, upper_ref)):
            total = dot(parts, ref[...].reshape(exp_dev * width, hidden)).astype(BF)
            for piece in range(size // PIECE):
                out_refs[which * per + first // PIECE + piece][...] = total[
                    piece * PIECE : (piece + 1) * PIECE
                ]


def down_kernel(lay, rows, chunk, adds, step_ref, meta_ref, down_ref, table_ref, *refs):
    exp_dev, hidden, width = down_ref.shape
    per = rows // PIECE
    refs = list(refs)
    before_ref = refs.pop(0) if adds else None
    summed, (out_ref, held_ref) = refs[: 2 * per], refs[2 * per :]
    base = step_ref[1]
    counts = meta_ref[...]
    high, low = starts_of(counts, lay)
    ends = ends_of(counts, lay)
    lane = iota((8, lay.wide), 1)
    low = jnp.where(lane == lay.experts, -1.0, low)
    room = jnp.where(lane == lay.experts, 1.0, counts)
    high, low, room = (jnp.broadcast_to(v[0:1], (128, lay.wide)).astype(BF) for v in (high, low, room))
    shift = base.astype(F32)
    for first in range(0, rows, chunk):
        size = min(chunk, rows - first)
        pieces = range(first // PIECE, (first + size) // PIECE)
        gate = jnp.concatenate([summed[p][...] for p in pieces], axis=0).astype(F32)
        upper = jnp.concatenate([summed[per + p][...] for p in pieces], axis=0).astype(F32)
        inner = (gate / (1.0 + jnp.exp(-gate)) * upper).astype(BF)
        row = (iota((size, width), 0) + first).astype(F32) + shift
        result = dot(inner, down_ref[0])
        for w in range(1, exp_dev):
            result = jnp.where(row >= ends[w - 1], dot(inner, down_ref[w]), result)
        held_ref[first : first + size, :] = result.astype(BF)
    held = held_ref[...]
    step = lay.rows * 4 if lay.columns % 4 == 0 else lay.rows
    for top in range(0, lay.total, step):
        table = table_ref[top : top + step, :]
        target = 64.0 * dot_nt(table, high) + dot_nt(table, low)
        target = jnp.where(dot_nt(table, room) > 0.0, target, -1.0).astype(jnp.int32) - base
        blocks = []
        for left in range(0, rows, 128):
            wide = min(128, rows - left)
            blocks.append((target[:, :wide] == iota((step, wide), 1) + left).astype(F32).astype(BF))
        pick = jnp.concatenate(blocks, axis=1) if len(blocks) > 1 else blocks[0]
        placed = dot(pick, held)
        if adds:
            placed = placed + before_ref[top : top + step, :].astype(F32)
        out_ref[top : top + step, :] = placed.astype(BF)


def experts(lay, rows, chunk, me, base, before, received, w_gate, w_up, w_down):
    exp_dev, width, hidden = w_gate.shape
    per = rows // PIECE
    vmem = pl.BlockSpec(memory_space=pltpu.VMEM)
    smem = pl.BlockSpec(memory_space=pltpu.SMEM)
    step = jnp.stack([me, jnp.asarray(base, jnp.int32)])
    meta, loads, most, *parts = pl.pallas_call(
        functools.partial(up_kernel, lay, rows, chunk),
        out_shape=[
            jax.ShapeDtypeStruct((8, lay.wide), F32),
            jax.ShapeDtypeStruct((exp_dev,), jnp.int32),
            jax.ShapeDtypeStruct((1,), jnp.int32),
        ]
        + [jax.ShapeDtypeStruct((PIECE, hidden), BF)] * (2 * per),
        in_specs=[smem] + [vmem] * 4,
        out_specs=[vmem, smem, smem] + [vmem] * (2 * per),
        compiler_params=PARAMS,
        name="up",
    )(step, received, w_gate, w_up, jnp.asarray(lay.table.T, BF))
    summed = lax.psum(parts, "dp")
    adds = before is not None
    out = pl.pallas_call(
        functools.partial(down_kernel, lay, rows, min(chunk, 192), adds),
        out_shape=jax.ShapeDtypeStruct((lay.total, width), BF),
        in_specs=[smem] + [vmem] * (3 + adds + 2 * per),
        out_specs=vmem,
        scratch_shapes=[pltpu.VMEM((rows, width), BF)],
        compiler_params=PARAMS,
        name="down",
    )(step, meta, w_down, jnp.asarray(lay.table, BF), *([before] if adds else []), *summed)
    return out, loads, most[0]


def dispatch(lay, route_ids, tokens):
    tok_col, width = tokens.shape
    top_k = route_ids.shape[1]
    table = jnp.asarray(lay.table, BF)
    sending = pl.pallas_call(
        functools.partial(dispatch_kernel, lay),
        out_shape=jax.ShapeDtypeStruct((lay.total, width), BF),
        in_specs=[pl.BlockSpec(memory_space=pl.ANY)] * 3,
        out_specs=pl.BlockSpec(memory_space=pltpu.VMEM),
        scratch_shapes=[
            pltpu.VMEM((top_k, tok_col), jnp.int32),
            pltpu.VMEM((tok_col, width), BF),
            pltpu.VMEM(table.shape, BF),
            pltpu.SemaphoreType.DMA((3,)),
        ],
        compiler_params=PARAMS,
        name="dispatch",
    )(route_ids.T, tokens, table)
    return lax.all_to_all(
        sending.reshape(lay.columns, lay.rows, width), "expert", split_axis=0, concat_axis=0, tiled=True
    ).reshape(lay.total, width)


def body(tokens, route_ids, route_weights, w_gate, w_up, w_down):
    columns = lax.axis_size("expert")
    tok_col, top_k = route_ids.shape
    exp_dev = w_gate.shape[0]
    width = tokens.shape[1]
    capacity = min(tok_col, 3 * tok_col * top_k // (exp_dev * columns))
    lay = Layout(columns, capacity, exp_dev)
    received = dispatch(lay, route_ids, tokens)
    matrix = pl.pallas_call(
        functools.partial(mix_kernel, lay),
        out_shape=jax.ShapeDtypeStruct((tok_col, lay.total), BF),
        compiler_params=PARAMS,
        name="mix",
    )(route_ids.T, route_weights.T, jnp.asarray(lay.table.T, BF))
    me = lax.axis_index("expert").astype(jnp.int32)
    rows = min(ROWS, columns * exp_dev * capacity)
    expert_out, loads, most = experts(lay, rows, CHUNK, me, 0, None, received, w_gate, w_up, w_down)

    def more(carry):
        return carry[0] < most

    def further(carry):
        base, out = carry
        again = dispatch(lay, *lax.optimization_barrier((route_ids, tokens, base))[:2])
        out, _, _ = experts(lay, rows, CHUNK, me, base, out, again, w_gate, w_up, w_down)
        return base + rows, out

    _, expert_out = lax.while_loop(more, further, (jnp.int32(rows), expert_out))
    returned = lax.all_to_all(
        expert_out.reshape(columns, lay.rows, width), "expert", split_axis=0, concat_axis=0, tiled=True
    ).reshape(lay.total, width)
    combined = pl.pallas_call(
        combine_kernel,
        out_shape=jax.ShapeDtypeStruct((tok_col, width), BF),
        compiler_params=PARAMS,
        name="combine",
    )(matrix, returned)
    return combined, loads


def solution(mesh):
    placed = (
        P("expert", "dp"),
        P("expert", None),
        P("expert", None),
        P("expert", "dp", None),
        P("expert", "dp", None),
        P("expert", None, "dp"),
    )
    return jax.shard_map(
        body,
        mesh=mesh,
        in_specs=placed,
        out_specs=(P("expert", "dp"), P("expert")),
        check_vma=False,
    )
```

```python
import functools

import jax
import jax.numpy as jnp
import numpy as np
from jax import lax
from jax.experimental import pallas as pl
from jax.experimental.pallas import tpu as pltpu
from jax.sharding import PartitionSpec as P

BF = jnp.bfloat16
F32 = jnp.float32
PIECE = 16
ROWS = 576
CHUNK = 576
NT = (((1,), (1,)), ((), ()))
PARAMS = pltpu.CompilerParams(vmem_limit_bytes=24 * 1024 * 1024)


def dot(a, b):
    return jnp.dot(a, b, preferred_element_type=F32)


def dot_nt(a, b):
    return lax.dot_general(a, b, NT, preferred_element_type=F32)


def iota(shape, dim):
    return lax.broadcasted_iota(jnp.int32, shape, dim)


FREE, COUNTS = 90, 100


class Layout:
    def __init__(self, columns, capacity, exp_dev):
        self.columns, self.capacity, self.exp_dev = columns, capacity, exp_dev
        self.sub = -(-(capacity + 1) // 8) * 8
        self.rows = -(-(self.sub * exp_dev) // 16) * 16
        self.total = columns * self.rows
        self.experts = columns * exp_dev
        self.wide = -(-(self.experts + 1) // 128) * 128
        row = np.arange(self.total)
        group, place = row // self.rows, row % self.rows
        within = np.minimum(place // self.sub, exp_dev - 1)
        at = place - within * self.sub
        at = np.where(at < capacity, at, np.where((at == capacity) & (within == 0), COUNTS, FREE))
        table = np.zeros((self.total, self.wide), np.float32)
        table[row, within * columns + group] = 1.0
        table[:, self.experts] = -at
        self.table = table

    def parts(self):
        groups = next(n for n in (8, 4, 2, 1) if self.columns % n == 0)
        size = self.rows * groups
        return [pl.ds(top, size) for top in range(0, self.total, size)]

    def expert_ids(self, shape, dim):
        at = iota(shape, dim)
        ids = at * self.exp_dev
        for w in range(1, self.exp_dev):
            ids = ids - jnp.where(at >= w * self.columns, self.experts - 1, 0)
        return ids


def chosen(ids_ref, lay):
    top_k, tokens = ids_ref.shape
    ids = ids_ref[...]
    of = lay.expert_ids((lay.experts, tokens), 0)
    chose = jnp.zeros((lay.experts, tokens), F32)
    for s in range(top_k):
        chose = chose + (ids[s : s + 1, :] == of).astype(F32)
    before = (iota((tokens, tokens), 0) < iota((tokens, tokens), 1)).astype(F32).astype(BF)
    rank = dot(chose.astype(BF), before)
    return chose, jnp.where(chose > 0, rank, -1.0)


def dispatch_kernel(lay, ids_from, tokens_from, table_from, out_to, ids_ref, tokens_ref, table_ref, out_ref, sems):
    copies = [
        pltpu.make_async_copy(ids_from, ids_ref, sems.at[0]),
        pltpu.make_async_copy(tokens_from, tokens_ref, sems.at[1]),
        pltpu.make_async_copy(table_from, table_ref, sems.at[2]),
    ]
    for copy in copies:
        copy.start()
    copies[0].wait()
    tokens, width = tokens_ref.shape
    real = -(-tokens // 8) * 8
    chose, slot = chosen(ids_ref, lay)
    counts = dot_nt(jnp.ones((8, tokens), BF), chose.astype(BF))
    counts = jnp.concatenate([counts, jnp.zeros((8, width - lay.experts), F32)], axis=1)
    copies[1].wait()
    extended = [tokens_ref[...].astype(F32), counts]
    if real > tokens:
        extended.insert(1, jnp.zeros((real - tokens, width), F32))
    extended = jnp.concatenate(extended, axis=0).astype(BF)
    extra = jnp.where(iota((lay.experts, real + 8 - tokens), 1) == real - tokens, float(COUNTS), -1.0)
    slot = jnp.concatenate([slot, extra], axis=1)
    ones = (iota((lay.wide - lay.experts, real + 8), 0) == 0).astype(F32)
    slot = jnp.concatenate([slot, ones], axis=0).astype(BF)
    copies[2].wait()
    copies = []
    for part in lay.parts():
        pick = (dot(table_ref[part, :], slot) == 0.0).astype(F32).astype(BF)
        out_ref[part, :] = dot(pick, extended).astype(BF)
        copies.append(pltpu.make_async_copy(out_ref.at[part], out_to.at[part], sems.at[3 + len(copies)]))
        copies[-1].start()
    for copy in copies:
        copy.wait()


def mix_kernel(lay, ids_ref, weights_ref, across_ref, out_ref):
    top_k, tokens = ids_ref.shape
    ids = ids_ref[...]
    mix = weights_ref[...].astype(BF).astype(F32)
    _, slot = chosen(ids_ref, lay)
    of = lay.expert_ids((lay.experts, tokens), 0)
    weight = jnp.zeros((lay.experts, tokens), F32)
    for s in range(top_k):
        weight = weight + jnp.where(ids[s : s + 1, :] == of, mix[s : s + 1, :], 0.0)
    rest = (tokens, lay.wide - lay.experts)
    slot = jnp.concatenate([slot.T, (iota(rest, 1) == 0).astype(F32)], axis=1).astype(BF)
    weight = jnp.concatenate([weight.T, jnp.zeros(rest, F32)], axis=1).astype(BF)
    across = across_ref[...]
    out_ref[...] = jnp.where(dot(slot, across) == 0.0, dot(weight, across), 0.0).astype(BF)


def combine_kernel(matrix_ref, back_ref, out_ref):
    out_ref[...] = dot(matrix_ref[...], back_ref[...]).astype(BF)


def starts_of(counts, lay):
    i, k = iota((lay.wide, lay.wide), 0), iota((lay.wide, lay.wide), 1)
    start = dot(counts.astype(BF), (i < k).astype(F32).astype(BF))
    start = jnp.where(iota(start.shape, 1) < lay.experts, start, 0.0)
    high = jnp.floor(start * (1.0 / 64.0))
    return high, start - 64.0 * high


def ends_of(counts, lay):
    lane = iota((1, lay.wide), 1)
    return [
        jnp.sum(jnp.where(lane < (w + 1) * lay.columns, counts[0:1], 0.0), axis=1, keepdims=True)
        for w in range(lay.exp_dev)
    ]


def up_kernel(lay, rows, chunk, step_ref, x_ref, gate_ref, upper_ref, across_ref, meta_ref, loads_ref, most_ref, *out_refs):
    exp_dev, width, hidden = gate_ref.shape
    per = rows // PIECE
    me, base = step_ref[0], step_ref[1]
    x = x_ref[...]
    across = across_ref[...]
    of_group = jnp.where(
        across_ref[lay.experts : lay.experts + 16, :].astype(F32)[0:1, :] == float(-COUNTS),
        across_ref[0 : lay.columns, :].astype(F32),
        0.0,
    ).astype(BF)
    every = dot(of_group, x).astype(BF)
    own = []
    for w in range(exp_dev):
        lane = (iota((8, width), 1) == w * lay.columns + me).astype(F32).astype(BF)
        own.append(dot_nt(lane, every))
    own.append(jnp.zeros((8, lay.wide - lay.experts), F32))
    counts = jnp.concatenate(own, axis=1)
    meta_ref[...] = counts
    high, low = starts_of(counts, lay)
    ends = ends_of(counts, lay)
    lane, row = iota((8, lay.wide), 1), iota((8, lay.wide), 0)
    low = jnp.where(lane == lay.experts, -1.0, low)
    room = jnp.where(lane == lay.experts, 1.0, counts)
    terms = jnp.where(row == 0, high, jnp.where(row == 1, low, room)).astype(BF)
    spread = dot(terms, across)
    target = jnp.where(spread[2:3] > 0.0, 64.0 * spread[0:1] + spread[1:2], -1.0)
    target = target.astype(jnp.int32) - base
    loads = dot(jnp.ones((8, lay.columns), BF), every)[0:1]
    begin = 0.0
    for w in range(exp_dev):
        loads_ref[w] = (jnp.sum(ends[w]) - begin).astype(jnp.int32)
        begin = jnp.sum(ends[w])
    lanes = iota((1, width), 1)
    full = loads
    for w in range(1, exp_dev):
        full = full + pltpu.roll(loads, width - w * lay.columns, axis=1)
    most_ref[0] = jnp.max(jnp.where(lanes < lay.columns, full, 0.0)).astype(jnp.int32)
    shift = base.astype(F32)
    for first in range(0, rows, chunk):
        size = min(chunk, rows - first)
        pick = (iota((size, lay.total), 0) + first == target).astype(F32).astype(BF)
        picked = dot(pick, x)
        row = (iota((size, width), 0) + first).astype(F32) + shift
        begin = jnp.zeros((1, 1), F32)
        parts = []
        for w in range(exp_dev):
            parts.append(jnp.where((row >= begin) & (row < ends[w]), picked, 0.0).astype(BF))
            begin = ends[w]
        parts = jnp.concatenate(parts, axis=1)
        for which, ref in enumerate((gate_ref, upper_ref)):
            total = dot(parts, ref[...].reshape(exp_dev * width, hidden)).astype(BF)
            for piece in range(size // PIECE):
                out_refs[which * per + first // PIECE + piece][...] = total[
                    piece * PIECE : (piece + 1) * PIECE
                ]


def down_kernel(lay, rows, chunk, adds, step_ref, meta_ref, down_from, table_from, *refs):
    exp_dev, hidden, width = down_from.shape
    per = rows // PIECE
    refs = list(refs)
    before_ref = refs.pop(0) if adds else None
    summed, (out_to, held_ref, down_ref, table_ref, out_ref, sems) = refs[: 2 * per], refs[2 * per :]
    arriving = [
        pltpu.make_async_copy(down_from, down_ref, sems.at[0]),
        pltpu.make_async_copy(table_from, table_ref, sems.at[1]),
    ]
    for copy in arriving:
        copy.start()
    base = step_ref[1]
    counts = meta_ref[...]
    high, low = starts_of(counts, lay)
    ends = ends_of(counts, lay)
    lane = iota((8, lay.wide), 1)
    low = jnp.where(lane == lay.experts, -1.0, low)
    room = jnp.where(lane == lay.experts, 1.0, counts)
    high, low, room = (jnp.broadcast_to(v[0:1], (128, lay.wide)).astype(BF) for v in (high, low, room))
    shift = base.astype(F32)
    for first in range(0, rows, chunk):
        size = min(chunk, rows - first)
        pieces = range(first // PIECE, (first + size) // PIECE)
        gate = jnp.concatenate([summed[p][...] for p in pieces], axis=0).astype(F32)
        upper = jnp.concatenate([summed[per + p][...] for p in pieces], axis=0).astype(F32)
        inner = (gate / (1.0 + jnp.exp(-gate)) * upper).astype(BF)
        row = (iota((size, width), 0) + first).astype(F32) + shift
        if first == 0:
            arriving[0].wait()
        result = dot(inner, down_ref[0])
        for w in range(1, exp_dev):
            result = jnp.where(row >= ends[w - 1], dot(inner, down_ref[w]), result)
        held_ref[first : first + size, :] = result.astype(BF)
    held = held_ref[...]
    arriving[1].wait()
    leaving = []
    for part in lay.parts():
        step = part.size
        table = table_ref[part, :]
        target = 64.0 * dot_nt(table, high) + dot_nt(table, low)
        target = jnp.where(dot_nt(table, room) > 0.0, target, -1.0).astype(jnp.int32) - base
        blocks = []
        for left in range(0, rows, 128):
            wide = min(128, rows - left)
            blocks.append((target[:, :wide] == iota((step, wide), 1) + left).astype(F32).astype(BF))
        pick = jnp.concatenate(blocks, axis=1) if len(blocks) > 1 else blocks[0]
        placed = dot(pick, held)
        if adds:
            placed = placed + before_ref[part, :].astype(F32)
        out_ref[part, :] = placed.astype(BF)
        leaving.append(pltpu.make_async_copy(out_ref.at[part], out_to.at[part], sems.at[2 + len(leaving)]))
        leaving[-1].start()
    for copy in leaving:
        copy.wait()


def experts(lay, rows, chunk, me, base, before, received, w_gate, w_up, w_down):
    exp_dev, width, hidden = w_gate.shape
    per = rows // PIECE
    vmem = pl.BlockSpec(memory_space=pltpu.VMEM)
    smem = pl.BlockSpec(memory_space=pltpu.SMEM)
    anywhere = pl.BlockSpec(memory_space=pl.ANY)
    step = jnp.stack([me, jnp.asarray(base, jnp.int32)])
    meta, loads, most, *parts = pl.pallas_call(
        functools.partial(up_kernel, lay, rows, chunk),
        out_shape=[
            jax.ShapeDtypeStruct((8, lay.wide), F32),
            jax.ShapeDtypeStruct((exp_dev,), jnp.int32),
            jax.ShapeDtypeStruct((1,), jnp.int32),
        ]
        + [jax.ShapeDtypeStruct((PIECE, hidden), BF)] * (2 * per),
        in_specs=[smem] + [vmem] * 4,
        out_specs=[vmem, smem, smem] + [vmem] * (2 * per),
        compiler_params=PARAMS,
        name="up",
    )(step, received, w_gate, w_up, jnp.asarray(lay.table.T, BF))
    summed = lax.psum(parts, "dp")
    adds = before is not None
    out = pl.pallas_call(
        functools.partial(down_kernel, lay, rows, min(chunk, 192), adds),
        out_shape=jax.ShapeDtypeStruct((lay.total, width), BF),
        in_specs=[smem, vmem, anywhere, anywhere] + [vmem] * (adds + 2 * per),
        out_specs=anywhere,
        scratch_shapes=[
            pltpu.VMEM((rows, width), BF),
            pltpu.VMEM(w_down.shape, BF),
            pltpu.VMEM(lay.table.shape, BF),
            pltpu.VMEM((lay.total, width), BF),
            pltpu.SemaphoreType.DMA((2 + len(lay.parts()),)),
        ],
        compiler_params=PARAMS,
        name="down",
    )(step, meta, w_down, jnp.asarray(lay.table, BF), *([before] if adds else []), *summed)
    return out, loads, most[0]


def dispatch(lay, route_ids, tokens):
    tok_col, width = tokens.shape
    top_k = route_ids.shape[1]
    table = jnp.asarray(lay.table, BF)
    sending = pl.pallas_call(
        functools.partial(dispatch_kernel, lay),
        out_shape=jax.ShapeDtypeStruct((lay.total, width), BF),
        in_specs=[pl.BlockSpec(memory_space=pl.ANY)] * 3,
        out_specs=pl.BlockSpec(memory_space=pl.ANY),
        scratch_shapes=[
            pltpu.VMEM((top_k, tok_col), jnp.int32),
            pltpu.VMEM((tok_col, width), BF),
            pltpu.VMEM(table.shape, BF),
            pltpu.VMEM((lay.total, width), BF),
            pltpu.SemaphoreType.DMA((3 + len(lay.parts()),)),
        ],
        compiler_params=PARAMS,
        name="dispatch",
    )(route_ids.T, tokens, table)
    return lax.all_to_all(
        sending.reshape(lay.columns, lay.rows, width), "expert", split_axis=0, concat_axis=0, tiled=True
    ).reshape(lay.total, width)


def body(tokens, route_ids, route_weights, w_gate, w_up, w_down):
    columns = lax.axis_size("expert")
    tok_col, top_k = route_ids.shape
    exp_dev = w_gate.shape[0]
    width = tokens.shape[1]
    capacity = min(tok_col, 3 * tok_col * top_k // (exp_dev * columns))
    lay = Layout(columns, capacity, exp_dev)
    received = dispatch(lay, route_ids, tokens)
    matrix = pl.pallas_call(
        functools.partial(mix_kernel, lay),
        out_shape=jax.ShapeDtypeStruct((tok_col, lay.total), BF),
        compiler_params=PARAMS,
        name="mix",
    )(route_ids.T, route_weights.T, jnp.asarray(lay.table.T, BF))
    me = lax.axis_index("expert").astype(jnp.int32)
    rows = min(ROWS, columns * exp_dev * capacity)
    expert_out, loads, most = experts(lay, rows, CHUNK, me, 0, None, received, w_gate, w_up, w_down)

    def more(carry):
        return carry[0] < most

    def further(carry):
        base, out = carry
        again = dispatch(lay, *lax.optimization_barrier((route_ids, tokens, base))[:2])
        out, _, _ = experts(lay, rows, CHUNK, me, base, out, again, w_gate, w_up, w_down)
        return base + rows, out

    _, expert_out = lax.while_loop(more, further, (jnp.int32(rows), expert_out))
    returned = lax.all_to_all(
        expert_out.reshape(columns, lay.rows, width), "expert", split_axis=0, concat_axis=0, tiled=True
    ).reshape(lay.total, width)
    combined = pl.pallas_call(
        combine_kernel,
        out_shape=jax.ShapeDtypeStruct((tok_col, width), BF),
        compiler_params=PARAMS,
        name="combine",
    )(matrix, returned)
    return combined, loads


def solution(mesh):
    placed = (
        P("expert", "dp"),
        P("expert", None),
        P("expert", None),
        P("expert", "dp", None),
        P("expert", "dp", None),
        P("expert", None, "dp"),
    )
    return jax.shard_map(
        body,
        mesh=mesh,
        in_specs=placed,
        out_specs=(P("expert", "dp"), P("expert")),
        check_vma=False,
    )
```

```python
import functools

import jax
import jax.numpy as jnp
import numpy as np
from jax import lax
from jax.experimental import pallas as pl
from jax.experimental.pallas import tpu as pltpu
from jax.sharding import PartitionSpec as P

BF = jnp.bfloat16
F32 = jnp.float32
PIECE = 16
LEAST = 65
ROWS = 576
CHUNK = 576
NT = (((1,), (1,)), ((), ()))
PARAMS = pltpu.CompilerParams(vmem_limit_bytes=24 * 1024 * 1024)


def pieces_of(rows):
    units = 2 * (rows // PIECE)
    pairs = max(0, min(units - LEAST, units // 2 - 2))
    cut = []
    for which in range(2):
        first = 0
        mine = (pairs + 1 - which) // 2
        while first < rows:
            size = 2 * PIECE if mine > 0 and first + 2 * PIECE <= rows else PIECE
            mine -= size > PIECE
            cut.append((which, first, size))
            first += size
    return cut


def dot(a, b):
    return jnp.dot(a, b, preferred_element_type=F32)


def dot_nt(a, b):
    return lax.dot_general(a, b, NT, preferred_element_type=F32)


def iota(shape, dim):
    return lax.broadcasted_iota(jnp.int32, shape, dim)


FREE, COUNTS = 90, 100


class Layout:
    def __init__(self, columns, capacity, exp_dev):
        self.columns, self.capacity, self.exp_dev = columns, capacity, exp_dev
        self.sub = -(-(capacity + 1) // 8) * 8
        self.rows = -(-(self.sub * exp_dev) // 16) * 16
        self.total = columns * self.rows
        self.experts = columns * exp_dev
        self.wide = -(-(self.experts + 1) // 128) * 128
        row = np.arange(self.total)
        group, place = row // self.rows, row % self.rows
        within = np.minimum(place // self.sub, exp_dev - 1)
        at = place - within * self.sub
        at = np.where(at < capacity, at, np.where((at == capacity) & (within == 0), COUNTS, FREE))
        table = np.zeros((self.total, self.wide), np.float32)
        table[row, within * columns + group] = 1.0
        table[:, self.experts] = -at
        self.table = table

    def parts(self):
        groups = next(n for n in (8, 4, 2, 1) if self.columns % n == 0)
        size = self.rows * groups
        return [pl.ds(top, size) for top in range(0, self.total, size)]

    def expert_ids(self, shape, dim):
        at = iota(shape, dim)
        ids = at * self.exp_dev
        for w in range(1, self.exp_dev):
            ids = ids - jnp.where(at >= w * self.columns, self.experts - 1, 0)
        return ids


def chosen(ids_ref, lay):
    top_k, tokens = ids_ref.shape
    ids = ids_ref[...]
    of = lay.expert_ids((lay.experts, tokens), 0)
    chose = jnp.zeros((lay.experts, tokens), F32)
    for s in range(top_k):
        chose = chose + (ids[s : s + 1, :] == of).astype(F32)
    before = (iota((tokens, tokens), 0) < iota((tokens, tokens), 1)).astype(F32).astype(BF)
    rank = dot(chose.astype(BF), before)
    return chose, jnp.where(chose > 0, rank, -1.0)


def dispatch_kernel(lay, ids_from, tokens_from, table_from, out_to, ids_ref, tokens_ref, table_ref, out_ref, sems):
    copies = [
        pltpu.make_async_copy(ids_from, ids_ref, sems.at[0]),
        pltpu.make_async_copy(tokens_from, tokens_ref, sems.at[1]),
        pltpu.make_async_copy(table_from, table_ref, sems.at[2]),
    ]
    for copy in copies:
        copy.start()
    copies[0].wait()
    tokens, width = tokens_ref.shape
    real = -(-tokens // 8) * 8
    chose, slot = chosen(ids_ref, lay)
    counts = dot_nt(jnp.ones((8, tokens), BF), chose.astype(BF))
    counts = jnp.concatenate([counts, jnp.zeros((8, width - lay.experts), F32)], axis=1)
    copies[1].wait()
    extended = [tokens_ref[...].astype(F32), counts]
    if real > tokens:
        extended.insert(1, jnp.zeros((real - tokens, width), F32))
    extended = jnp.concatenate(extended, axis=0).astype(BF)
    extra = jnp.where(iota((lay.experts, real + 8 - tokens), 1) == real - tokens, float(COUNTS), -1.0)
    slot = jnp.concatenate([slot, extra], axis=1)
    ones = (iota((lay.wide - lay.experts, real + 8), 0) == 0).astype(F32)
    slot = jnp.concatenate([slot, ones], axis=0).astype(BF)
    copies[2].wait()
    copies = []
    for part in lay.parts():
        pick = (dot(table_ref[part, :], slot) == 0.0).astype(F32).astype(BF)
        out_ref[part, :] = dot(pick, extended).astype(BF)
        copies.append(pltpu.make_async_copy(out_ref.at[part], out_to.at[part], sems.at[3 + len(copies)]))
        copies[-1].start()
    for copy in copies:
        copy.wait()


def mix_kernel(lay, ids_ref, weights_ref, across_ref, out_ref):
    top_k, tokens = ids_ref.shape
    ids = ids_ref[...]
    mix = weights_ref[...].astype(BF).astype(F32)
    _, slot = chosen(ids_ref, lay)
    of = lay.expert_ids((lay.experts, tokens), 0)
    weight = jnp.zeros((lay.experts, tokens), F32)
    for s in range(top_k):
        weight = weight + jnp.where(ids[s : s + 1, :] == of, mix[s : s + 1, :], 0.0)
    rest = (tokens, lay.wide - lay.experts)
    slot = jnp.concatenate([slot.T, (iota(rest, 1) == 0).astype(F32)], axis=1).astype(BF)
    weight = jnp.concatenate([weight.T, jnp.zeros(rest, F32)], axis=1).astype(BF)
    across = across_ref[...]
    out_ref[...] = jnp.where(dot(slot, across) == 0.0, dot(weight, across), 0.0).astype(BF)


def combine_kernel(matrix_ref, back_ref, out_ref):
    out_ref[...] = dot(matrix_ref[...], back_ref[...]).astype(BF)


def starts_of(counts, lay):
    i, k = iota((lay.wide, lay.wide), 0), iota((lay.wide, lay.wide), 1)
    start = dot(counts.astype(BF), (i < k).astype(F32).astype(BF))
    start = jnp.where(iota(start.shape, 1) < lay.experts, start, 0.0)
    high = jnp.floor(start * (1.0 / 64.0))
    return high, start - 64.0 * high


def ends_of(counts, lay):
    lane = iota((1, lay.wide), 1)
    return [
        jnp.sum(jnp.where(lane < (w + 1) * lay.columns, counts[0:1], 0.0), axis=1, keepdims=True)
        for w in range(lay.exp_dev)
    ]


def up_kernel(lay, rows, chunk, step_ref, x_ref, gate_ref, upper_ref, across_ref, meta_ref, loads_ref, most_ref, *out_refs):
    exp_dev, width, hidden = gate_ref.shape
    me, base = step_ref[0], step_ref[1]
    x = x_ref[...]
    across = across_ref[...]
    of_group = jnp.where(
        across_ref[lay.experts : lay.experts + 16, :].astype(F32)[0:1, :] == float(-COUNTS),
        across_ref[0 : lay.columns, :].astype(F32),
        0.0,
    ).astype(BF)
    every = dot(of_group, x).astype(BF)
    own = []
    for w in range(exp_dev):
        lane = (iota((8, width), 1) == w * lay.columns + me).astype(F32).astype(BF)
        own.append(dot_nt(lane, every))
    own.append(jnp.zeros((8, lay.wide - lay.experts), F32))
    counts = jnp.concatenate(own, axis=1)
    meta_ref[...] = counts
    high, low = starts_of(counts, lay)
    ends = ends_of(counts, lay)
    lane, row = iota((8, lay.wide), 1), iota((8, lay.wide), 0)
    low = jnp.where(lane == lay.experts, -1.0, low)
    room = jnp.where(lane == lay.experts, 1.0, counts)
    terms = jnp.where(row == 0, high, jnp.where(row == 1, low, room)).astype(BF)
    spread = dot(terms, across)
    target = jnp.where(spread[2:3] > 0.0, 64.0 * spread[0:1] + spread[1:2], -1.0)
    target = target.astype(jnp.int32) - base
    loads = dot(jnp.ones((8, lay.columns), BF), every)[0:1]
    begin = 0.0
    for w in range(exp_dev):
        loads_ref[w] = (jnp.sum(ends[w]) - begin).astype(jnp.int32)
        begin = jnp.sum(ends[w])
    lanes = iota((1, width), 1)
    full = loads
    for w in range(1, exp_dev):
        full = full + pltpu.roll(loads, width - w * lay.columns, axis=1)
    most_ref[0] = jnp.max(jnp.where(lanes < lay.columns, full, 0.0)).astype(jnp.int32)
    shift = base.astype(F32)
    for first in range(0, rows, chunk):
        size = min(chunk, rows - first)
        pick = (iota((size, lay.total), 0) + first == target).astype(F32).astype(BF)
        picked = dot(pick, x)
        row = (iota((size, width), 0) + first).astype(F32) + shift
        begin = jnp.zeros((1, 1), F32)
        parts = []
        for w in range(exp_dev):
            parts.append(jnp.where((row >= begin) & (row < ends[w]), picked, 0.0).astype(BF))
            begin = ends[w]
        parts = jnp.concatenate(parts, axis=1)
        for which, ref in enumerate((gate_ref, upper_ref)):
            total = dot(parts, ref[...].reshape(exp_dev * width, hidden)).astype(BF)
            for out_ref, (of, top, tall) in zip(out_refs, pieces_of(rows)):
                if of == which and first <= top < first + size:
                    out_ref[...] = total[top - first : top - first + tall]


def down_kernel(lay, rows, chunk, adds, step_ref, meta_ref, down_from, table_from, *refs):
    exp_dev, hidden, width = down_from.shape
    cut = pieces_of(rows)
    refs = list(refs)
    before_ref = refs.pop(0) if adds else None
    summed, (out_to, held_ref, down_ref, table_ref, out_ref, sems) = refs[: len(cut)], refs[len(cut) :]
    arriving = [
        pltpu.make_async_copy(down_from, down_ref, sems.at[0]),
        pltpu.make_async_copy(table_from, table_ref, sems.at[1]),
    ]
    for copy in arriving:
        copy.start()
    base = step_ref[1]
    counts = meta_ref[...]
    high, low = starts_of(counts, lay)
    ends = ends_of(counts, lay)
    lane = iota((8, lay.wide), 1)
    low = jnp.where(lane == lay.experts, -1.0, low)
    room = jnp.where(lane == lay.experts, 1.0, counts)
    high, low, room = (jnp.broadcast_to(v[0:1], (128, lay.wide)).astype(BF) for v in (high, low, room))
    shift = base.astype(F32)
    for first in range(0, rows, chunk):
        size = min(chunk, rows - first)
        gate, upper = (
            jnp.concatenate(
                [r[...] for r, (of, top, _) in zip(summed, cut) if of == which and first <= top < first + size],
                axis=0,
            ).astype(F32)
            for which in range(2)
        )
        inner = (gate / (1.0 + jnp.exp(-gate)) * upper).astype(BF)
        row = (iota((size, width), 0) + first).astype(F32) + shift
        if first == 0:
            arriving[0].wait()
        result = dot(inner, down_ref[0])
        for w in range(1, exp_dev):
            result = jnp.where(row >= ends[w - 1], dot(inner, down_ref[w]), result)
        held_ref[first : first + size, :] = result.astype(BF)
    held = held_ref[...]
    arriving[1].wait()
    leaving = []
    for part in lay.parts():
        step = part.size
        table = table_ref[part, :]
        target = 64.0 * dot_nt(table, high) + dot_nt(table, low)
        target = jnp.where(dot_nt(table, room) > 0.0, target, -1.0).astype(jnp.int32) - base
        blocks = []
        for left in range(0, rows, 128):
            wide = min(128, rows - left)
            blocks.append((target[:, :wide] == iota((step, wide), 1) + left).astype(F32).astype(BF))
        pick = jnp.concatenate(blocks, axis=1) if len(blocks) > 1 else blocks[0]
        placed = dot(pick, held)
        if adds:
            placed = placed + before_ref[part, :].astype(F32)
        out_ref[part, :] = placed.astype(BF)
        leaving.append(pltpu.make_async_copy(out_ref.at[part], out_to.at[part], sems.at[2 + len(leaving)]))
        leaving[-1].start()
    for copy in leaving:
        copy.wait()


def experts(lay, rows, chunk, me, base, before, received, w_gate, w_up, w_down):
    exp_dev, width, hidden = w_gate.shape
    cut = pieces_of(rows)
    vmem = pl.BlockSpec(memory_space=pltpu.VMEM)
    smem = pl.BlockSpec(memory_space=pltpu.SMEM)
    anywhere = pl.BlockSpec(memory_space=pl.ANY)
    step = jnp.stack([me, jnp.asarray(base, jnp.int32)])
    meta, loads, most, *parts = pl.pallas_call(
        functools.partial(up_kernel, lay, rows, chunk),
        out_shape=[
            jax.ShapeDtypeStruct((8, lay.wide), F32),
            jax.ShapeDtypeStruct((exp_dev,), jnp.int32),
            jax.ShapeDtypeStruct((1,), jnp.int32),
        ]
        + [jax.ShapeDtypeStruct((tall, hidden), BF) for _, _, tall in cut],
        in_specs=[smem] + [vmem] * 4,
        out_specs=[vmem, smem, smem] + [vmem] * len(cut),
        compiler_params=PARAMS,
        name="up",
    )(step, received, w_gate, w_up, jnp.asarray(lay.table.T, BF))
    summed = lax.psum(parts, "dp")
    adds = before is not None
    out = pl.pallas_call(
        functools.partial(down_kernel, lay, rows, min(chunk, 192), adds),
        out_shape=jax.ShapeDtypeStruct((lay.total, width), BF),
        in_specs=[smem, vmem, anywhere, anywhere] + [vmem] * (adds + len(cut)),
        out_specs=anywhere,
        scratch_shapes=[
            pltpu.VMEM((rows, width), BF),
            pltpu.VMEM(w_down.shape, BF),
            pltpu.VMEM(lay.table.shape, BF),
            pltpu.VMEM((lay.total, width), BF),
            pltpu.SemaphoreType.DMA((2 + len(lay.parts()),)),
        ],
        compiler_params=PARAMS,
        name="down",
    )(step, meta, w_down, jnp.asarray(lay.table, BF), *([before] if adds else []), *summed)
    return out, loads, most[0]


def dispatch(lay, route_ids, tokens):
    tok_col, width = tokens.shape
    top_k = route_ids.shape[1]
    table = jnp.asarray(lay.table, BF)
    sending = pl.pallas_call(
        functools.partial(dispatch_kernel, lay),
        out_shape=jax.ShapeDtypeStruct((lay.total, width), BF),
        in_specs=[pl.BlockSpec(memory_space=pl.ANY)] * 3,
        out_specs=pl.BlockSpec(memory_space=pl.ANY),
        scratch_shapes=[
            pltpu.VMEM((top_k, tok_col), jnp.int32),
            pltpu.VMEM((tok_col, width), BF),
            pltpu.VMEM(table.shape, BF),
            pltpu.VMEM((lay.total, width), BF),
            pltpu.SemaphoreType.DMA((3 + len(lay.parts()),)),
        ],
        compiler_params=PARAMS,
        name="dispatch",
    )(route_ids.T, tokens, table)
    return lax.all_to_all(
        sending.reshape(lay.columns, lay.rows, width), "expert", split_axis=0, concat_axis=0, tiled=True
    ).reshape(lay.total, width)


def body(tokens, route_ids, route_weights, w_gate, w_up, w_down):
    columns = lax.axis_size("expert")
    tok_col, top_k = route_ids.shape
    exp_dev = w_gate.shape[0]
    width = tokens.shape[1]
    capacity = min(tok_col, 3 * tok_col * top_k // (exp_dev * columns))
    lay = Layout(columns, capacity, exp_dev)
    received = dispatch(lay, route_ids, tokens)
    matrix = pl.pallas_call(
        functools.partial(mix_kernel, lay),
        out_shape=jax.ShapeDtypeStruct((tok_col, lay.total), BF),
        compiler_params=PARAMS,
        name="mix",
    )(route_ids.T, route_weights.T, jnp.asarray(lay.table.T, BF))
    me = lax.axis_index("expert").astype(jnp.int32)
    rows = min(ROWS, columns * exp_dev * capacity)
    expert_out, loads, most = experts(lay, rows, CHUNK, me, 0, None, received, w_gate, w_up, w_down)

    def more(carry):
        return carry[0] < most

    def further(carry):
        base, out = carry
        again = dispatch(lay, *lax.optimization_barrier((route_ids, tokens, base))[:2])
        out, _, _ = experts(lay, rows, CHUNK, me, base, out, again, w_gate, w_up, w_down)
        return base + rows, out

    _, expert_out = lax.while_loop(more, further, (jnp.int32(rows), expert_out))
    returned = lax.all_to_all(
        expert_out.reshape(columns, lay.rows, width), "expert", split_axis=0, concat_axis=0, tiled=True
    ).reshape(lay.total, width)
    combined = pl.pallas_call(
        combine_kernel,
        out_shape=jax.ShapeDtypeStruct((tok_col, width), BF),
        compiler_params=PARAMS,
        name="combine",
    )(matrix, returned)
    return combined, loads


def solution(mesh):
    placed = (
        P("expert", "dp"),
        P("expert", None),
        P("expert", None),
        P("expert", "dp", None),
        P("expert", "dp", None),
        P("expert", None, "dp"),
    )
    return jax.shard_map(
        body,
        mesh=mesh,
        in_specs=placed,
        out_specs=(P("expert", "dp"), P("expert")),
        check_vma=False,
    )
```
